32 devices in a mesh: parts: 2 (over y), band: 16 (over z, x, core).
Axes of the slice: x: 2, y: 2, z: 4, core: 2. Of those that a mesh axis runs over, the one named last changes fastest.
Arguments:
- sky_image: bfloat16 [8192, 16384], P(('parts', 'band')), parts along dimension 0, may hold values from -6 to 6
- tile_band: int32 [2048, 1], P(('parts', 'band')), parts along dimension 0, may hold values from 0 to 15; in each aligned block of 64 rows (0 to 63, 64 to 127, ...) at most 8 rows name the same one
- tile_place: int32 [2048], P(('parts', 'band')), parts along dimension 0, may hold values from 0 to 2047
- counts: int32 [32, 64], P(('parts', 'band')), parts along dimension 0, may hold values from 1 to 128, 4096 in all within a row
- kernel: bfloat16 [2048, 128, 128], P(('parts', 'band')), parts along dimension 0, may hold values from -1.5 to 1.5
- observed: bfloat16 [2048, 2, 128], P(('parts', 'band')), parts along dimension 0, may hold values from -24 to 24
Outputs:
- gradient: bfloat16 [8192, 16384], P(('parts', 'band')), parts along dimension 0
The draws below stay inside these ranges and needn't reach their ends.
There are 2 independent parts, one for each index of `parts`. The reference program is written for one: setup_inputs(seed, part) draws one part's arguments, and reference() takes and returns one part's arrays. A program takes and returns all parts, laid end to end along the dimension named above; each array names one. Nothing has to cross between parts.
Inputs may be any that keep to these rules, and one draw needn't show every extreme that they name: `tile_band`: no band is named by more than 8 slots of one index of band, and some index of band names one band exactly 8 times. The 64 counts of one index of band sum to 4096, the largest exactly 128.
All inputs are finite; a program needn't handle non-finite values.
Results may differ from the reference program's by a relative error of at most 0.015.
Values may be sent and summed in bfloat16 or wider, within the bound.
No kernel may reach another device: no remote copies, remote signals or barrier semaphores. Data moves between devices by JAX's collectives and lax.ppermute only.
A program may use at most 512 MiB of HBM per device.

```python
import math
import jax
import jax.numpy as jnp
import numpy as np
from jax import lax

N = 16384
RADIX = 128
FACET = 4096
TILE = 64
VIS_SLOT = 128
TILES_DEV = 64
CAP = 8
LIVE_DEV = 4096
SLOTS = 1024
TILES_BAND = 2048
N_BAND = 16


def plant(values, rng, least, top_value):
    longest = values.shape.index(max(values.shape))
    spots = []
    for shift in (0, 1):
        where = [jax.random.randint(jax.random.fold_in(rng, axis), (), 0, length) for axis, length in enumerate(values.shape)]
        where[longest] = (where[longest] + shift) % values.shape[longest]
        spots.append(tuple(where))
    return values.at[spots[0]].set(least).at[spots[1]].set(top_value)


def block_levels(key, extent, cuts, low, top_value):
    def one(position, parts):
        draws = jax.random.uniform(jax.random.fold_in(jax.random.fold_in(key, 6), position), (parts,), jnp.float32, low / len(cuts), top_value / len(cuts))
        return jnp.repeat(jnp.exp(draws), extent[position] // parts).reshape((-1,) + (1,) * (len(extent) - position - 1))

    loudness = one(*cuts[0])
    for cut in cuts[1:]:
        loudness = loudness * one(*cut)
    return loudness


def split_up(amount, total, most, skew):
    weights = [(1 << 20) // math.isqrt(grade ** skew) + 1 for grade in range(2, amount + 1)]
    surplus, given = total - most - (amount - 1), [1] * (amount - 1)
    while surplus > 0:
        candidates = [i for i in range(amount - 1) if given[i] < most]
        mass, remaining = sum([weights[i] for i in candidates]), surplus
        for i in candidates:
            more = min(most - given[i], max(1, remaining * weights[i] // mass), surplus)
            given[i] = given[i] + more
            surplus = surplus - more
    return np.array([most] + given)


def ragged_sizes(stream_key, count, total, reach, skew):
    if count == 2:
        one = jax.random.randint(stream_key, (), max(1, total - reach), min(reach, total - 1) + 1)
        return jnp.stack([one, total - one])
    lengths = jnp.asarray(split_up(count, total, reach, skew), jnp.int32)
    twos = (count - 1) // 2
    donor, taker = lengths[1:1 + 2 * twos:2], lengths[2:2 + 2 * twos:2]
    margin = jnp.minimum(donor - 1, reach - taker)
    passed = jax.random.randint(jax.random.fold_in(stream_key, 1), (twos,), 0, 1 << 20) % (margin + 1)
    lengths = lengths.at[1:1 + 2 * twos:2].set(donor - passed).at[2:2 + 2 * twos:2].set(taker + passed)
    return lengths[jax.random.permutation(jax.random.fold_in(stream_key, 2), count)]


def deal_out(own_key, own, number, rows, count, top, most, skew):
    sequence = jax.random.permutation(own_key, count)
    heavy_load, common = load_shares(count, rows * top, most, skew, True), load_shares(count, rows * top, most, skew, False)
    places = jnp.arange(count)

    def named(sizes, offset_by):
        used = int((sizes > 0).sum())
        fixed = max(1, used // 4)
        shifted = fixed + (places - fixed + offset_by * (used - fixed)) % max(1, count - fixed)
        return jnp.zeros((count,), jnp.int32).at[sequence[jnp.where(places < fixed, places, shifted)]].set(jnp.asarray(sizes, jnp.int32))

    sizes = jnp.where(number % 4 == 0, named(heavy_load, number // 4), named(common, number - number // 4 - 1))
    mixed = jax.random.permutation(jax.random.fold_in(own, 3), count)
    giver, taker = mixed[0:count // 2 * 2:2], mixed[1:count // 2 * 2:2]
    room = jnp.minimum(sizes[giver] - 1, most - sizes[taker]) // 2
    room = jnp.where((giver == sequence[0]) | (taker == sequence[0]) | (sizes[taker] == 0), 0, jnp.maximum(room, 0))
    shifted = jax.random.randint(jax.random.fold_in(own, 4), (count // 2,), 0, 1 << 20) % (room + 1)
    sizes = sizes.at[giver].add(-shifted).at[taker].add(shifted)
    labels = jnp.searchsorted(jnp.cumsum(sizes), jnp.arange(rows * top), side="right").astype(jnp.int32)
    listing = labels.reshape(top, rows).T
    listing = listing[jax.random.permutation(jax.random.fold_in(own, 1), rows)]
    offset_by = jax.random.randint(jax.random.fold_in(own, 2), (rows, 1), 0, top)
    return jnp.take_along_axis(listing, (jnp.arange(top)[None, :] + offset_by) % top, axis=1)


def load_shares(number_of, total, bound, lean, full):
    loads = [(1 << 20) // math.isqrt(grade ** lean) + 1 for grade in range(1, number_of + 1)]
    largest = bound if full else min(bound, max(-(-total // number_of), total * loads[0] // sum(loads)))
    least = 1 if total - largest >= number_of - 1 else 0
    given, rest = [largest] + [least] * (number_of - 1), total - largest - least * (number_of - 1)
    while rest > 0:
        candidates = [i for i in range(1, number_of) if given[i] < largest] or [i for i in range(1, number_of) if given[i] < bound]
        pool, budget = sum([loads[i] for i in candidates]), rest
        for i in candidates:
            extra = min(bound - given[i], max(1, budget * loads[i] // pool), rest)
            given[i] = given[i] + extra
            rest = rest - extra
    return np.array(given)


def bell_draw(rng, shape, scale, bound, cuts=(), kind=jnp.bfloat16):
    gain = block_levels(rng, shape, cuts, -0.22, 0.18) if cuts else 1.0
    result = jax.random.normal(rng, shape, jnp.float32) * scale * gain
    return jnp.minimum(jnp.maximum(result, -bound), bound).astype(kind)


def setup_inputs(seed: int = 0, part: int = 0) -> dict:
    streams_of = jax.random.split(jax.random.key(seed), 7)
    part_keys = jax.random.split(jax.random.fold_in(streams_of[6], part), 7)
    sky_image = bell_draw(part_keys[0], (FACET, N), 1.0, 6.0, ((0, 16),))
    tile_band_keys = jax.random.split(jax.random.fold_in(part_keys[1], 1), SLOTS // TILES_DEV)
    tile_band_turns = jax.random.permutation(jax.random.fold_in(part_keys[1], 3), SLOTS // TILES_DEV)
    tile_band = jax.vmap(lambda own, number: deal_out(jax.random.fold_in(part_keys[1], 2), own, number, TILES_DEV, N_BAND, 1, CAP, 2))(tile_band_keys, tile_band_turns).reshape((SLOTS, 1))
    tile_place = plant(jax.random.randint(part_keys[2], (SLOTS,), 0, TILES_BAND), jax.random.fold_in(part_keys[2], 1), 0, TILES_BAND - 1).astype(jnp.int32)
    counts = jax.vmap(lambda own: ragged_sizes(own, TILES_DEV, LIVE_DEV, VIS_SLOT, 2))(jax.random.split(part_keys[3], N_BAND)).reshape((N_BAND, TILES_DEV)).astype(jnp.int32)
    kernel = bell_draw(part_keys[4], (SLOTS, VIS_SLOT, 2 * TILE), (TILE // 4) ** -0.5, 1.5, ((0, 16),))
    observed = bell_draw(part_keys[5], (SLOTS, 2, VIS_SLOT), 4.0, 24.0, ((0, 16),))
    return dict(sky_image=sky_image, tile_band=tile_band, tile_place=tile_place, counts=counts, kernel=kernel, observed=observed)


def contract(pattern, table_part, data_part):
    return jnp.einsum(pattern, table_part.astype(jnp.float32), data_part.astype(jnp.float32))


def dft_tables(orient):
    table_index = jnp.arange(RADIX, dtype=jnp.int32)
    product = (table_index[:, None] * table_index[None, :]) % RADIX
    table_angle = product.astype(jnp.float32) * (2.0 * math.pi / RADIX)
    return jnp.cos(table_angle).astype(jnp.bfloat16), (orient * jnp.sin(table_angle)).astype(jnp.bfloat16)


def twiddle(orient):
    table_index = jnp.arange(RADIX, dtype=jnp.int32)
    product = table_index[:, None] * table_index[None, :]
    table_angle = product.astype(jnp.float32) * (2.0 * math.pi / (RADIX * RADIX))
    return jnp.cos(table_angle), orient * jnp.sin(table_angle)


def along_last(part_real, part_imag, orient, used_in, used_out, real_out):
    cos_table, sin_table = dft_tables(orient)
    twist_cos, twist_sin = twiddle(orient)
    batch_rows = part_real.shape[0]
    head_cos = cos_table[:, :used_in]
    head_sin = sin_table[:, :used_in]
    real_cube = part_real.reshape(batch_rows, used_in, RADIX)
    first_real = contract("kn,bnm->bkm", head_cos, real_cube)
    first_imag = contract("kn,bnm->bkm", head_sin, real_cube)
    if part_imag is not None:
        imag_cube = part_imag.reshape(batch_rows, used_in, RADIX)
        first_real = first_real - contract("kn,bnm->bkm", head_sin, imag_cube)
        first_imag = first_imag + contract("kn,bnm->bkm", head_cos, imag_cube)
    middle_real = ((first_real * twist_cos - first_imag * twist_sin) / RADIX).astype(jnp.bfloat16)
    middle_imag = ((first_real * twist_sin + first_imag * twist_cos) / RADIX).astype(jnp.bfloat16)
    tail_cos = cos_table[:used_out]
    tail_sin = sin_table[:used_out]
    final_real = contract("jm,bkm->bjk", tail_cos, middle_real) - contract("jm,bkm->bjk", tail_sin, middle_imag)
    final_real = final_real.reshape(batch_rows, used_out * RADIX)
    if real_out:
        return final_real
    final_imag = contract("jm,bkm->bjk", tail_cos, middle_imag) + contract("jm,bkm->bjk", tail_sin, middle_real)
    return final_real, final_imag.reshape(batch_rows, used_out * RADIX)


def slot_gradient(tile_real, tile_imag, kernel, observed, counts):
    kernel_v = kernel[:, :, :TILE]
    kernel_u = kernel[:, :, TILE:]
    inner_real = contract("sab,sjb->sja", tile_real, kernel_u)
    inner_imag = contract("sab,sjb->sja", tile_imag, kernel_u)
    weight_v = kernel_v.astype(jnp.float32)
    model_real = jnp.sum(weight_v * inner_real, axis=2)
    model_imag = jnp.sum(weight_v * inner_imag, axis=2)
    live_mask = jnp.arange(VIS_SLOT, dtype=jnp.int32)[None, :] < counts[:, None]
    resid_real = jnp.where(live_mask, observed[:, 0].astype(jnp.float32) - model_real, jnp.zeros_like(model_real))
    resid_imag = jnp.where(live_mask, observed[:, 1].astype(jnp.float32) - model_imag, jnp.zeros_like(model_imag))
    weighted_real = (weight_v * resid_real[:, :, None]).astype(jnp.bfloat16)
    weighted_imag = (weight_v * resid_imag[:, :, None]).astype(jnp.bfloat16)
    grad_real = contract("sja,sjb->sab", weighted_real, kernel_u)
    grad_imag = contract("sja,sjb->sab", weighted_imag, kernel_u)
    return grad_real, grad_imag


def reference(sky_image, tile_band, tile_place, counts, kernel, observed):
    half_cells = N // 2
    band_cols = half_cells // N_BAND
    tiles_across = band_cols // TILE
    tiles_wide = half_cells // TILE
    facet_blocks = FACET // RADIX
    block_rows = min(FACET, 512)
    block_cols = min(half_cells, 256)
    col_blocks = half_cells // block_cols

    def forward_rows(rows_block):
        return along_last(rows_block, None, -1.0, RADIX, RADIX // 2, False)

    spec_real, spec_imag = lax.map(forward_rows, sky_image.reshape(FACET // block_rows, block_rows, N))
    spec_real = spec_real.reshape(FACET, half_cells).astype(jnp.bfloat16)
    spec_imag = spec_imag.reshape(FACET, half_cells).astype(jnp.bfloat16)

    def by_columns(part_real, part_imag, orient, used_in, used_out):
        width = part_real.shape[1]

        def one_block(block_pair):
            return along_last(block_pair[0], block_pair[1], orient, used_in, used_out, False)

        out_real, out_imag = lax.map(one_block, (part_real.reshape(col_blocks, block_cols, width),
                                                 part_imag.reshape(col_blocks, block_cols, width)))
        return out_real.reshape(half_cells, used_out * RADIX), out_imag.reshape(half_cells, used_out * RADIX)

    grid_real, grid_imag = by_columns(spec_real.T, spec_imag.T, -1.0, facet_blocks, RADIX)
    grid_real = grid_real.astype(jnp.bfloat16)
    grid_imag = grid_imag.astype(jnp.bfloat16)

    def as_tiles(field):
        return field.reshape(tiles_wide, TILE, N // TILE, TILE).transpose(2, 0, 3, 1)

    def from_tiles(field):
        return field.transpose(1, 3, 0, 2).reshape(half_cells, N)

    owner_band = tile_band[:, 0]
    tile_row = tile_place // tiles_across
    tile_col = owner_band * tiles_across + tile_place % tiles_across
    slot_real = as_tiles(grid_real)[tile_row, tile_col]
    slot_imag = as_tiles(grid_imag)[tile_row, tile_col]
    slot_total = N_BAND * TILES_DEV
    slot_counts = counts.reshape(slot_total)
    block_slots = min(slot_total, 1024)
    slot_blocks = slot_total // block_slots

    def slot_block(block_items):
        return slot_gradient(block_items[0], block_items[1], block_items[2], block_items[3], block_items[4])

    grad_real, grad_imag = lax.map(slot_block, (
        slot_real.reshape(slot_blocks, block_slots, TILE, TILE),
        slot_imag.reshape(slot_blocks, block_slots, TILE, TILE),
        kernel.reshape(slot_blocks, block_slots, VIS_SLOT, 2 * TILE),
        observed.reshape(slot_blocks, block_slots, 2, VIS_SLOT),
        slot_counts.reshape(slot_blocks, block_slots)))
    grad_real = grad_real.reshape(slot_total, TILE, TILE)
    grad_imag = grad_imag.reshape(slot_total, TILE, TILE)
    zero_tiles = jnp.zeros((N // TILE, tiles_wide, TILE, TILE), jnp.float32)
    sum_real = zero_tiles.at[tile_row, tile_col].add(grad_real)
    sum_imag = zero_tiles.at[tile_row, tile_col].add(grad_imag)
    half_real = from_tiles(sum_real).astype(jnp.bfloat16)
    half_imag = from_tiles(sum_imag).astype(jnp.bfloat16)
    col_real, col_imag = by_columns(half_real, half_imag, 1.0, RADIX, facet_blocks)
    col_real = col_real.astype(jnp.bfloat16).T
    col_imag = col_imag.astype(jnp.bfloat16).T

    def inverse_rows(block_pair):
        return along_last(block_pair[0], block_pair[1], 1.0, RADIX // 2, RADIX, True)

    image_out = lax.map(inverse_rows, (col_real.reshape(FACET // block_rows, block_rows, half_cells),
                                       col_imag.reshape(FACET // block_rows, block_rows, half_cells)))
    return image_out.reshape(FACET, N).astype(jnp.bfloat16)
```

```python
import math

import jax
import jax.numpy as jnp
import numpy as np
from jax import lax
from jax.experimental import pallas as pl
from jax.experimental.pallas import tpu as pltpu
from jax.sharding import PartitionSpec as P

RADIX = 128
SIDE = RADIX * RADIX
TILE = 64
HALF_BLOCKS = RADIX // 2
TILE_ROWS = SIDE // TILE
VIS_SLOT = 128
ROW_ALIGN = 16
ROWS_STEP = 16
STEP_PAIRS = 4
STEP_SLOTS = 2 * STEP_PAIRS
F32 = jnp.float32
BF16 = jnp.bfloat16
NT = (((1,), (1,)), ((), ()))
MIB = 1 << 20


def dot(a, b):
    return jnp.dot(a, b, preferred_element_type=F32)


def dot_nt(a, b):
    return lax.dot_general(a, b, NT, preferred_element_type=F32)


def radix_tables():
    index = np.arange(RADIX)
    angle = (index[:, None] * index[None, :] % RADIX) * (2.0 * math.pi / RADIX)
    turn = (index[:, None] * index[None, :]) * (2.0 * math.pi / SIDE)
    twist = np.concatenate([np.cos(turn), np.sin(turn)]) / RADIX
    return np.cos(angle), np.sin(angle), twist.astype(np.float32)


def whole(shape, space=pltpu.VMEM):
    return pl.BlockSpec(shape, lambda *_: (0,) * len(shape), memory_space=space)


def rows_forward_kernel(sky_ref, head_ref, twist_ref, tail_ref, out_ref, apart, done):
    for a in range(RADIX):
        apart[pl.ds(a, ROWS_STEP, stride=RADIX), :] = sky_ref[:, a * RADIX:(a + 1) * RADIX].astype(F32)

    def two_rows(i, _):
        first = apart[pl.ds(pl.multiple_of(2 * i * RADIX, RADIX), RADIX), :]
        second = apart[pl.ds(pl.multiple_of((2 * i + 1) * RADIX, RADIX), RADIX), :]
        mixed = dot(head_ref[...], jnp.concatenate([first, second], axis=1).astype(BF16))
        twist_cos, twist_sin = twist_ref[:RADIX], twist_ref[RADIX:]
        for side in range(2):
            part = slice(side * RADIX, (side + 1) * RADIX)
            by_cos, by_sin = mixed[:RADIX, part], mixed[RADIX:, part]
            middle_real = by_cos * twist_cos - by_sin * twist_sin
            middle_imag = -(by_cos * twist_sin + by_sin * twist_cos)
            middle = jnp.concatenate([middle_real, middle_imag], axis=1).astype(BF16)
            done[pl.ds(pl.multiple_of((2 * i + side) * RADIX, RADIX), RADIX), :] = dot_nt(tail_ref[...], middle)
        return 0

    lax.fori_loop(0, ROWS_STEP // 2, two_rows, 0, unroll=2)
    for j in range(HALF_BLOCKS):
        real = done[pl.ds(j, ROWS_STEP, stride=RADIX), :]
        imag = done[pl.ds(HALF_BLOCKS + j, ROWS_STEP, stride=RADIX), :]
        out_ref[j] = jnp.concatenate([real, imag], axis=1).astype(BF16)


def rows_forward(sky):
    rows = sky.shape[0]
    cos, sin, twist = radix_tables()
    head = jnp.asarray(np.concatenate([cos, sin]), BF16)
    tail = jnp.asarray(np.block([[cos[:HALF_BLOCKS], sin[:HALF_BLOCKS]], [-sin[:HALF_BLOCKS], cos[:HALF_BLOCKS]]]), BF16)
    return pl.pallas_call(
        rows_forward_kernel,
        grid=(rows // ROWS_STEP,),
        in_specs=[pl.BlockSpec((ROWS_STEP, SIDE), lambda i: (i, 0)), whole(head.shape), whole(twist.shape), whole(tail.shape)],
        out_specs=pl.BlockSpec((HALF_BLOCKS, ROWS_STEP, 2 * RADIX), lambda i: (0, i, 0)),
        out_shape=jax.ShapeDtypeStruct((HALF_BLOCKS, rows, 2 * RADIX), BF16),
        scratch_shapes=[pltpu.VMEM((ROWS_STEP * RADIX, RADIX), F32), pltpu.VMEM((ROWS_STEP * RADIX, RADIX), F32)],
        compiler_params=pltpu.CompilerParams(vmem_limit_bytes=24 * MIB),
        cost_estimate=pl.CostEstimate(flops=rows * RADIX * RADIX * 1024, bytes_accessed=rows * SIDE * 4, transcendentals=0),
        name="rows_forward",
    )(sky, head, jnp.asarray(twist), tail)


def rows_inverse_kernel(in_ref, head_ref, twist_ref, tail_ref, out_ref, apart, done):
    for j in range(HALF_BLOCKS):
        apart[pl.ds(j, ROWS_STEP, stride=HALF_BLOCKS), :] = in_ref[j, :, :RADIX].astype(F32)
        apart[pl.ds(ROWS_STEP * HALF_BLOCKS + j, ROWS_STEP, stride=HALF_BLOCKS), :] = in_ref[j, :, RADIX:].astype(F32)

    def one_row(y, _):
        real = apart[pl.ds(pl.multiple_of(y * HALF_BLOCKS, HALF_BLOCKS), HALF_BLOCKS), :]
        imag = apart[pl.ds(pl.multiple_of((ROWS_STEP + y) * HALF_BLOCKS, HALF_BLOCKS), HALF_BLOCKS), :]
        mixed = dot(head_ref[...], jnp.concatenate([real, imag], axis=1).astype(BF16))
        twist_cos, twist_sin = twist_ref[:RADIX], twist_ref[RADIX:]
        first_real = mixed[:RADIX, :RADIX] - mixed[RADIX:, RADIX:]
        first_imag = mixed[RADIX:, :RADIX] + mixed[:RADIX, RADIX:]
        middle_real = first_real * twist_cos - first_imag * twist_sin
        middle_imag = first_real * twist_sin + first_imag * twist_cos
        middle = jnp.concatenate([middle_real, middle_imag], axis=1).astype(BF16)
        done[pl.ds(pl.multiple_of(y * RADIX, RADIX), RADIX), :] = dot_nt(tail_ref[...], middle)
        return 0

    lax.fori_loop(0, ROWS_STEP, one_row, 0, unroll=4)
    for j in range(RADIX):
        out_ref[:, j * RADIX:(j + 1) * RADIX] = done[pl.ds(j, ROWS_STEP, stride=RADIX), :].astype(BF16)


def rows_inverse(columns):
    rows = columns.shape[1]
    cos, sin, twist = radix_tables()
    head = jnp.asarray(np.concatenate([cos[:, :HALF_BLOCKS], sin[:, :HALF_BLOCKS]]), BF16)
    tail = jnp.asarray(np.concatenate([cos, -sin], axis=1), BF16)
    return pl.pallas_call(
        rows_inverse_kernel,
        grid=(rows // ROWS_STEP,),
        in_specs=[pl.BlockSpec((HALF_BLOCKS, ROWS_STEP, 2 * RADIX), lambda i: (0, i, 0)), whole(head.shape), whole(twist.shape), whole(tail.shape)],
        out_specs=pl.BlockSpec((ROWS_STEP, SIDE), lambda i: (i, 0)),
        out_shape=jax.ShapeDtypeStruct((rows, SIDE), BF16),
        scratch_shapes=[pltpu.VMEM((2 * ROWS_STEP * HALF_BLOCKS, RADIX), F32), pltpu.VMEM((ROWS_STEP * RADIX, RADIX), F32)],
        compiler_params=pltpu.CompilerParams(vmem_limit_bytes=24 * MIB),
        cost_estimate=pl.CostEstimate(flops=rows * RADIX * RADIX * 1024, bytes_accessed=rows * SIDE * 4, transcendentals=0),
        name="rows_inverse",
    )(columns, head, jnp.asarray(twist), tail)


def pack_kernel(place_ref, half_ref, last_ref, weights_ref, out_ref):
    lane = lax.broadcasted_iota(jnp.int32, (VIS_SLOT, 2 * TILE), 1)

    def put(slot):
        block = weights_ref[slot].astype(F32)
        swapped = pltpu.roll(block, TILE, 1)
        keep = (lane * 0 + half_ref[slot]) == 1
        start = pl.multiple_of(place_ref[slot], ROW_ALIGN)
        out_ref[pl.ds(start, VIS_SLOT), :] = jnp.where(keep, block, swapped).astype(BF16)

    def one(slot, _):
        @pl.when(slot != last_ref[0])
        def _():
            put(slot)
        return 0

    lax.fori_loop(0, weights_ref.shape[0], one, 0)
    put(last_ref[0])


def pack(place, half, last, weights, pack_rows):
    return pl.pallas_call(
        pack_kernel,
        in_specs=[pl.BlockSpec(memory_space=pltpu.SMEM)] * 3 + [pl.BlockSpec(memory_space=pltpu.VMEM)],
        out_specs=pl.BlockSpec(memory_space=pltpu.VMEM),
        out_shape=jax.ShapeDtypeStruct((pack_rows, 2 * TILE), BF16),
        compiler_params=pltpu.CompilerParams(vmem_limit_bytes=16 * MIB),
        cost_estimate=pl.CostEstimate(flops=0, bytes_accessed=4 * MIB, transcendentals=0),
        name="pack",
    )(place, half, last, weights)


def fetch(order_ref, start_ref, packed_ref, blocks, sems, step, buffer):
    copies = []
    for i in range(STEP_SLOTS):
        slot = order_ref[step * STEP_SLOTS + i]
        start = pl.multiple_of(start_ref[slot], ROW_ALIGN)
        copies.append(pltpu.make_async_copy(packed_ref.at[pl.ds(start, VIS_SLOT), :], blocks.at[buffer, i], sems.at[buffer, i]))
    return copies


def over_steps(order_ref, start_ref, steps, packed_ref, blocks, sems, work):
    for copy in fetch(order_ref, start_ref, packed_ref, blocks, sems, 0, 0):
        copy.start()

    def step_body(step, _):
        buffer = lax.rem(step, 2)

        @pl.when(step + 1 < steps)
        def _():
            for copy in fetch(order_ref, start_ref, packed_ref, blocks, sems, step + 1, 1 - buffer):
                copy.start()

        for copy in fetch(order_ref, start_ref, packed_ref, blocks, sems, step, buffer):
            copy.wait()
        work(step, buffer)
        return 0

    lax.fori_loop(0, steps, step_body, 0)


def model_kernel(order_ref, start_ref, row_ref, half_ref, block_ref, steps_ref, table_ref, spectrum_ref, pick_ref, packed_ref, out_ref, blocks, sems):
    lane = lax.broadcasted_iota(jnp.int32, (VIS_SLOT, 2 * TILE), 1) // TILE

    def work(step, buffer):
        for pair in range(STEP_PAIRS):
            slots = [order_ref[step * STEP_SLOTS + 2 * pair + i] for i in range(2)]
            columns = spectrum_ref[block_ref[step * STEP_PAIRS + pair]]
            tables = jnp.concatenate([table_ref[row_ref[slot]] for slot in slots], axis=0)
            turned = dot(tables, columns)
            for i, slot in enumerate(slots):
                base = 2 * TILE * i
                by_cos, by_sin = turned[base:base + TILE], turned[base + TILE:base + 2 * TILE]
                tile_real = by_cos[:, :RADIX] + by_sin[:, RADIX:]
                tile_imag = by_cos[:, RADIX:] - by_sin[:, :RADIX]
                tile = jnp.concatenate([tile_real, tile_imag], axis=0).astype(BF16)
                weights = blocks[buffer, 2 * pair + i].astype(F32)
                along_u = lane == half_ref[slot]
                weights_u = jnp.where(along_u, weights, 0.0).astype(BF16)
                weights_v = jnp.where(along_u, pltpu.roll(weights, TILE, 1), weights)
                product = dot_nt(weights_u, tile) * weights_v
                high = product.astype(BF16)
                low = (product - high.astype(F32)).astype(BF16)
                summed = dot_nt(pick_ref[...], jnp.concatenate([high, low], axis=1))
                out_ref[slot] = summed[:2]

    over_steps(order_ref, start_ref, steps_ref[0], packed_ref, blocks, sems, work)


def model_parts(scalars, table, spectrum, packed, slot_rows):
    pick = np.zeros((16, 4 * TILE), np.float32)
    pick[0, :TILE] = pick[0, 2 * TILE:3 * TILE] = 1.0
    pick[1, TILE:2 * TILE] = pick[1, 3 * TILE:] = 1.0
    return pl.pallas_call(
        model_kernel,
        in_specs=[pl.BlockSpec(memory_space=pltpu.SMEM)] * 6 + [pl.BlockSpec(memory_space=pltpu.VMEM)] * 3 + [pl.BlockSpec(memory_space=pl.ANY)],
        out_specs=pl.BlockSpec(memory_space=pltpu.VMEM),
        out_shape=jax.ShapeDtypeStruct((slot_rows, 2, VIS_SLOT), F32),
        scratch_shapes=[pltpu.VMEM((2, STEP_SLOTS, VIS_SLOT, 2 * TILE), BF16), pltpu.SemaphoreType.DMA((2, STEP_SLOTS))],
        compiler_params=pltpu.CompilerParams(vmem_limit_bytes=52 * MIB),
        cost_estimate=pl.CostEstimate(flops=slot_rows * RADIX ** 3 * 6, bytes_accessed=64 * MIB, transcendentals=0),
        name="model",
    )(*scalars, table, spectrum, jnp.asarray(pick, BF16), packed)


def gradient_kernel(order_ref, start_ref, row_ref, half_ref, block_ref, steps_ref, table_ref, residual_ref, turn_ref, packed_ref, out_ref, total, blocks, sems):
    lane = lax.broadcasted_iota(jnp.int32, (VIS_SLOT, 2 * TILE), 1) // TILE

    def clear(j, _):
        total[j] = jnp.zeros(total.shape[1:], F32)
        return 0

    lax.fori_loop(0, HALF_BLOCKS, clear, 0)

    def work(step, buffer):
        for pair in range(STEP_PAIRS):
            slots = [order_ref[step * STEP_SLOTS + 2 * pair + i] for i in range(2)]
            tiles = []
            for i, slot in enumerate(slots):
                weights = blocks[buffer, 2 * pair + i]
                half = half_ref[slot]
                weights_u = jnp.where(lane == half, weights.astype(F32), 0.0).astype(BF16)
                turned_v = dot_nt(turn_ref[half], weights)
                residual = residual_ref[slot]
                weighted = jnp.concatenate([turned_v[:TILE] * residual[0:1], turned_v[TILE:] * residual[1:2]], axis=0)
                tile = dot(weighted.astype(BF16), weights_u)
                real, imag = tile[:TILE], tile[TILE:]
                tiles.append(jnp.concatenate([real, imag], axis=1))
                tiles.append(jnp.concatenate([-imag, real], axis=1))
            both = jnp.concatenate(tiles, axis=0).astype(BF16)
            tables = jnp.concatenate([table_ref[row_ref[slot]] for slot in slots], axis=1)
            block = block_ref[step * STEP_PAIRS + pair]
            total[block] = total[block] + dot(tables, both)

    over_steps(order_ref, start_ref, steps_ref[0], packed_ref, blocks, sems, work)

    def round_off(j, _):
        out_ref[j] = total[j].astype(BF16)
        return 0

    lax.fori_loop(0, HALF_BLOCKS, round_off, 0)


def gradient_columns(scalars, table, residual, packed, rows):
    turn = np.zeros((2, 2 * TILE, 2 * TILE), np.float32)
    for a in range(TILE):
        turn[0, [a, TILE + a], TILE + a] = 1.0
        turn[1, [a, TILE + a], a] = 1.0
    return pl.pallas_call(
        gradient_kernel,
        in_specs=[pl.BlockSpec(memory_space=pltpu.SMEM)] * 6 + [pl.BlockSpec(memory_space=pltpu.VMEM)] * 3 + [pl.BlockSpec(memory_space=pl.ANY)],
        out_specs=pl.BlockSpec(memory_space=pltpu.VMEM),
        out_shape=jax.ShapeDtypeStruct((HALF_BLOCKS, rows, 2 * RADIX), BF16),
        scratch_shapes=[
            pltpu.VMEM((HALF_BLOCKS, rows, 2 * RADIX), F32),
            pltpu.VMEM((2, STEP_SLOTS, VIS_SLOT, 2 * TILE), BF16),
            pltpu.SemaphoreType.DMA((2, STEP_SLOTS)),
        ],
        compiler_params=pltpu.CompilerParams(vmem_limit_bytes=56 * MIB),
        cost_estimate=pl.CostEstimate(flops=residual.shape[0] * RADIX ** 3 * 6, bytes_accessed=64 * MIB, transcendentals=0),
        name="gradient",
    )(*scalars, table, residual, jnp.asarray(turn, BF16), packed)


def column_tables(first_row, rows):
    y = first_row + jnp.arange(rows, dtype=jnp.int32)
    r = jnp.arange(TILE_ROWS, dtype=jnp.int32)
    a = jnp.arange(TILE, dtype=jnp.int32)
    coarse = (r[:, None] * y[None, :] % TILE_ROWS).astype(F32) * (2.0 * math.pi / TILE_ROWS)
    fine = (a[:, None] * y[None, :] % SIDE).astype(F32) * (2.0 * math.pi / SIDE)
    coarse_cos, coarse_sin = jnp.cos(coarse), jnp.sin(coarse)
    fine_cos, fine_sin = jnp.cos(fine) / RADIX, jnp.sin(fine) / RADIX
    with_cos = jnp.concatenate([fine_cos, fine_sin])
    with_sin = jnp.concatenate([fine_sin, -fine_cos])
    forward = coarse_cos[:, None, :] * with_cos[None] - coarse_sin[:, None, :] * with_sin[None]
    inverse = coarse_cos[:, :, None] * with_cos.T[None] - coarse_sin[:, :, None] * with_sin.T[None]
    return forward.astype(BF16), inverse.astype(BF16)


def pack_places(counts):
    padded = (counts + ROW_ALIGN - 1) // ROW_ALIGN * ROW_ALIGN
    slot = jnp.arange(counts.shape[1], dtype=jnp.int32)
    last = jnp.argmax(counts, axis=1).astype(jnp.int32)
    is_last = slot[None, :] == last[:, None]
    ahead = (slot[None, None, :] < slot[None, :, None]) & ~is_last[:, None, :] | (is_last[:, :, None] & ~is_last[:, None, :])
    return jnp.sum(jnp.where(ahead, padded[:, None, :], 0), axis=2), last


def spread(values, band_count):
    return lax.all_to_all(jnp.broadcast_to(values[None], (band_count,) + values.shape), "band", 0, 0, tiled=True)


def on_device(sky_image, tile_band, tile_place, counts, kernel, observed):
    band_count = lax.axis_size("band")
    rows = sky_image.shape[0]
    slots_here = tile_place.shape[0]
    slots_all = band_count * slots_here
    tiles_across = sky_image.shape[1] // 2 // band_count // TILE
    live_here = slots_here // 2 * VIS_SLOT
    pack_rows = (live_here + (slots_here - 1) * (ROW_ALIGN - 1)) // ROW_ALIGN * ROW_ALIGN

    tile_row = tile_place // tiles_across
    tile_col = tile_band[:, 0] * tiles_across + tile_place % tiles_across
    place, last = pack_places(counts)
    packed = lax.all_gather(pack(place[0], tile_col % 2, last, kernel, pack_rows), "band", tiled=True)

    every = spread(jnp.stack([tile_row, tile_col, counts[0]]), band_count)
    all_row, all_col, all_counts = (every[:, i].reshape(slots_all) for i in range(3))
    all_place, _ = pack_places(every[:, 2])
    all_start = (all_place + pack_rows * jnp.arange(band_count, dtype=jnp.int32)[:, None]).reshape(slots_all)
    all_block = all_col // 2

    spectrum = rows_forward(sky_image)
    forward_table, inverse_table = column_tables(lax.axis_index("band").astype(jnp.int32) * rows, rows)

    slot = jnp.arange(slots_all, dtype=jnp.int32)
    block = jnp.arange(HALF_BLOCKS, dtype=jnp.int32)
    in_block = jnp.sum((all_block[:, None] == block[None, :]).astype(jnp.int32), axis=0)
    pairs_of = (in_block + 1) // 2
    pairs_to = jnp.sum(jnp.where(block[None, :] <= block[:, None], pairs_of[None, :], 0), axis=1)
    rank = jnp.sum(((all_block[:, None] == all_block[None, :]) & (slot[None, :] < slot[:, None])).astype(jnp.int32), axis=1)
    first_pair = jnp.sum(jnp.where(block[None, :] < all_block[:, None], pairs_of[None, :], 0), axis=1)
    position = 2 * first_pair + rank
    steps_most = (slots_all + HALF_BLOCKS + STEP_SLOTS - 1) // STEP_SLOTS
    positions = jnp.arange(steps_most * STEP_SLOTS, dtype=jnp.int32)
    order = slots_all + jnp.sum(jnp.where(position[None, :] == positions[:, None], slot[None, :] - slots_all, 0), axis=1)
    pair_block = jnp.sum((pairs_to[None, :] <= positions[:steps_most * STEP_PAIRS, None]).astype(jnp.int32), axis=1)
    pair_block = jnp.minimum(pair_block, HALF_BLOCKS - 1)
    steps = (pairs_to[-1:] + STEP_PAIRS - 1) // STEP_PAIRS

    def spare(values):
        return jnp.pad(values, (0, 8))

    scalars = (order, spare(all_start), spare(all_row), spare(all_col % 2), pair_block, steps)
    parts = model_parts(scalars, forward_table, spectrum, packed, slots_all + 8)[:slots_all]
    parts = parts.reshape(band_count, slots_here, 2, VIS_SLOT)
    model = jnp.sum(lax.all_to_all(parts, "band", 0, 0, tiled=True), axis=0)
    live = jnp.arange(VIS_SLOT, dtype=jnp.int32)[None, None, :] < counts[0][:, None, None]
    residual = jnp.where(live, observed.astype(F32) - model, 0.0)
    residual = spread(residual, band_count).reshape(slots_all, 2, VIS_SLOT)
    residual = jnp.pad(residual, ((0, 8), (0, 0), (0, 0)))
    columns = gradient_columns(scalars, inverse_table, residual, packed, rows)
    return rows_inverse(columns)


def solution(mesh):
    return jax.shard_map(
        on_device,
        mesh=mesh,
        in_specs=(
            P(("parts", "band"), None),
            P(("parts", "band"), None),
            P(("parts", "band")),
            P(("parts", "band"), None),
            P(("parts", "band"), None, None),
            P(("parts", "band"), None, None),
        ),
        out_specs=P(("parts", "band"), None),
        check_vma=False,
    )
```

```python
import functools
import math

import jax
import jax.numpy as jnp
import numpy as np
from jax import lax
from jax.experimental import pallas as pl
from jax.experimental.pallas import tpu as pltpu
from jax.sharding import PartitionSpec as P

RADIX = 128
SIDE = RADIX * RADIX
TILE = 64
HALF_BLOCKS = RADIX // 2
TILE_ROWS = SIDE // TILE
VIS_SLOT = 128
ROW_PITCH = RADIX + 8
ROWS_STEP = 16
STEP_PAIRS = 8
STEP_SLOTS = 2 * STEP_PAIRS
BUFFERS = 4
TILES_PAIRS = 16
TILES_SLOTS = 2 * TILES_PAIRS
RESIDENT_BYTES = 16 << 20
F32 = jnp.float32
BF16 = jnp.bfloat16
NT = (((1,), (1,)), ((), ()))
MIB = 1 << 20


def dot(a, b):
    return jnp.dot(a, b, preferred_element_type=F32)


def dot_nt(a, b):
    return lax.dot_general(a, b, NT, preferred_element_type=F32)


def radix_tables():
    index = np.arange(RADIX)
    angle = (index[:, None] * index[None, :] % RADIX) * (2.0 * math.pi / RADIX)
    turn = (index[:, None] * index[None, :]) * (2.0 * math.pi / SIDE)
    twist = np.concatenate([np.cos(turn), np.sin(turn)]) / RADIX
    return np.cos(angle), np.sin(angle), twist.astype(np.float32)


def whole(shape, space=pltpu.VMEM):
    return pl.BlockSpec(shape, lambda *_: (0,) * len(shape), memory_space=space)


def two_by_two(apart, head_ref, tail_ref, done, twisted):
    def two_rows(i, _):
        first = apart[pl.ds(pl.multiple_of(2 * i * ROW_PITCH, 8), RADIX), :]
        second = apart[pl.ds(pl.multiple_of((2 * i + 1) * ROW_PITCH, 8), RADIX), :]
        mixed = dot(head_ref[...], jnp.concatenate([first, second], axis=1).astype(BF16))
        for side in range(2):
            part = slice(side * RADIX, (side + 1) * RADIX)
            middle = jnp.concatenate(twisted(mixed[:RADIX, part], mixed[RADIX:, part]), axis=1).astype(BF16)
            done[pl.ds(pl.multiple_of((2 * i + side) * ROW_PITCH, 8), RADIX), :] = dot_nt(tail_ref[...], middle)
        return 0

    lax.fori_loop(0, ROWS_STEP // 2, two_rows, 0, unroll=True)


def rows_forward_kernel(sky_ref, head_ref, twist_ref, tail_ref, out_ref, apart, done):
    for a in range(RADIX):
        apart[pl.ds(a, ROWS_STEP, stride=ROW_PITCH), :] = sky_ref[:, a * RADIX:(a + 1) * RADIX].astype(F32)

    def twisted(by_cos, by_sin):
        twist_cos, twist_sin = twist_ref[:RADIX], twist_ref[RADIX:]
        return [by_cos * twist_cos - by_sin * twist_sin, -(by_cos * twist_sin + by_sin * twist_cos)]

    two_by_two(apart, head_ref, tail_ref, done, twisted)
    for j in range(HALF_BLOCKS):
        real = done[pl.ds(j, ROWS_STEP, stride=ROW_PITCH), :]
        imag = done[pl.ds(HALF_BLOCKS + j, ROWS_STEP, stride=ROW_PITCH), :]
        out_ref[j] = jnp.concatenate([real, imag], axis=1).astype(BF16)


def rows_forward(sky):
    rows = sky.shape[0]
    cos, sin, twist = radix_tables()
    head = jnp.asarray(np.concatenate([cos, sin]), BF16)
    tail = jnp.asarray(np.block([[cos[:HALF_BLOCKS], sin[:HALF_BLOCKS]], [-sin[:HALF_BLOCKS], cos[:HALF_BLOCKS]]]), BF16)
    return pl.pallas_call(
        rows_forward_kernel,
        grid=(rows // ROWS_STEP,),
        in_specs=[pl.BlockSpec((ROWS_STEP, SIDE), lambda i: (i, 0)), whole(head.shape), whole(twist.shape), whole(tail.shape)],
        out_specs=pl.BlockSpec((HALF_BLOCKS, ROWS_STEP, 2 * RADIX), lambda i: (0, i, 0)),
        out_shape=jax.ShapeDtypeStruct((HALF_BLOCKS, rows, 2 * RADIX), BF16),
        scratch_shapes=[pltpu.VMEM((ROWS_STEP * ROW_PITCH, RADIX), F32), pltpu.VMEM((ROWS_STEP * ROW_PITCH, RADIX), F32)],
        compiler_params=pltpu.CompilerParams(vmem_limit_bytes=24 * MIB),
        cost_estimate=pl.CostEstimate(flops=rows * RADIX * RADIX * 1024, bytes_accessed=rows * SIDE * 4, transcendentals=0),
        name="rows_forward",
    )(sky, head, jnp.asarray(twist), tail)


def rows_inverse_kernel(in_ref, head_ref, twist_ref, tail_ref, out_ref, apart, done):
    for j in range(HALF_BLOCKS):
        apart[pl.ds(j, ROWS_STEP, stride=ROW_PITCH), :] = in_ref[j, :, :RADIX].astype(F32)
        apart[pl.ds(HALF_BLOCKS + j, ROWS_STEP, stride=ROW_PITCH), :] = in_ref[j, :, RADIX:].astype(F32)

    def twisted(real, imag):
        twist_cos, twist_sin = twist_ref[:RADIX], twist_ref[RADIX:]
        return [real * twist_cos - imag * twist_sin, real * twist_sin + imag * twist_cos]

    two_by_two(apart, head_ref, tail_ref, done, twisted)
    for j in range(RADIX):
        out_ref[:, j * RADIX:(j + 1) * RADIX] = done[pl.ds(j, ROWS_STEP, stride=ROW_PITCH), :].astype(BF16)


def rows_inverse(columns):
    rows = columns.shape[1]
    cos, sin, twist = radix_tables()
    used_cos, used_sin = cos[:, :HALF_BLOCKS], sin[:, :HALF_BLOCKS]
    head = jnp.asarray(np.block([[used_cos, -used_sin], [used_sin, used_cos]]), BF16)
    tail = jnp.asarray(np.concatenate([cos, -sin], axis=1), BF16)
    return pl.pallas_call(
        rows_inverse_kernel,
        grid=(rows // ROWS_STEP,),
        in_specs=[pl.BlockSpec((HALF_BLOCKS, ROWS_STEP, 2 * RADIX), lambda i: (0, i, 0)), whole(head.shape), whole(twist.shape), whole(tail.shape)],
        out_specs=pl.BlockSpec((ROWS_STEP, SIDE), lambda i: (i, 0)),
        out_shape=jax.ShapeDtypeStruct((rows, SIDE), BF16),
        scratch_shapes=[pltpu.VMEM((ROWS_STEP * ROW_PITCH, RADIX), F32), pltpu.VMEM((ROWS_STEP * ROW_PITCH, RADIX), F32)],
        compiler_params=pltpu.CompilerParams(vmem_limit_bytes=24 * MIB),
        cost_estimate=pl.CostEstimate(flops=rows * RADIX * RADIX * 1024, bytes_accessed=rows * SIDE * 4, transcendentals=0),
        name="rows_inverse",
    )(columns, head, jnp.asarray(twist), tail)


def pack_kernel(first_ref, weights_ref, observed_ref, out_ref, seen_ref, lined):
    column = lax.broadcasted_iota(jnp.int32, (8, VIS_SLOT), 1)

    def one(slot, _):
        first = first_ref[slot]
        lined[pl.ds(first, VIS_SLOT), :] = weights_ref[slot].astype(F32)
        tile, shift = first // VIS_SLOT, first % VIS_SLOT
        turned = pltpu.roll(observed_ref[slot], shift, 1)
        seen_ref[tile] = jnp.where(column >= shift, turned, seen_ref[tile])
        seen_ref[tile + 1] = turned
        return 0

    lax.fori_loop(0, weights_ref.shape[0], one, 0)
    for tile in range(out_ref.shape[0]):
        out_ref[tile] = lined[tile * VIS_SLOT:(tile + 1) * VIS_SLOT, :].T.astype(BF16)


def pack(first, weights, observed, tiles):
    return pl.pallas_call(
        pack_kernel,
        in_specs=[pl.BlockSpec(memory_space=pltpu.SMEM)] + [pl.BlockSpec(memory_space=pltpu.VMEM)] * 2,
        out_specs=[pl.BlockSpec(memory_space=pltpu.VMEM)] * 2,
        out_shape=[jax.ShapeDtypeStruct((tiles, 2 * TILE, VIS_SLOT), BF16), jax.ShapeDtypeStruct((tiles + 1, 8, VIS_SLOT), F32)],
        scratch_shapes=[pltpu.VMEM(((tiles + 1) * VIS_SLOT, 2 * TILE), F32)],
        compiler_params=pltpu.CompilerParams(vmem_limit_bytes=16 * MIB),
        cost_estimate=pl.CostEstimate(flops=0, bytes_accessed=4 * MIB, transcendentals=0),
        name="pack",
    )(first, weights, observed)


def tiles_kernel(order_ref, row_ref, block_ref, steps_ref, table_ref, spectrum_ref, out_ref, ready, sems):
    steps = (steps_ref[0] * STEP_PAIRS + TILES_PAIRS - 1) // TILES_PAIRS

    def leave(step, buffer):
        return pltpu.make_async_copy(ready.at[buffer], out_ref.at[pl.ds(step * TILES_SLOTS, TILES_SLOTS)], sems.at[buffer])

    def step_body(step, _):
        buffer = lax.rem(step, BUFFERS)

        @pl.when(step >= BUFFERS)
        def _():
            leave(step - BUFFERS, buffer).wait()

        for pair in range(TILES_PAIRS):
            slots = [order_ref[step * TILES_SLOTS + 2 * pair + i] for i in range(2)]
            columns = spectrum_ref[block_ref[step * TILES_PAIRS + pair]]
            tables = jnp.concatenate([table_ref[row_ref[slot]] for slot in slots], axis=0)
            turned = dot(tables, columns)
            for i in range(2):
                base = 2 * TILE * i
                by_cos, by_sin = turned[base:base + TILE], turned[base + TILE:base + 2 * TILE]
                ready[buffer, 2 * pair + i, :TILE] = (by_cos[:, :RADIX] + by_sin[:, RADIX:]).astype(BF16)
                ready[buffer, 2 * pair + i, TILE:] = (by_cos[:, RADIX:] - by_sin[:, :RADIX]).astype(BF16)
        leave(step, buffer).start()
        return 0

    lax.fori_loop(0, steps, step_body, 0)
    for back in range(BUFFERS, 0, -1):
        leave(steps - back, lax.rem(steps - back, BUFFERS)).wait()


def tile_parts(scalars, table, spectrum):
    order, window, low, high, row, half, block, steps = scalars
    return pl.pallas_call(
        tiles_kernel,
        in_specs=[pl.BlockSpec(memory_space=pltpu.SMEM)] * 4 + [pl.BlockSpec(memory_space=pltpu.VMEM)] * 2,
        out_specs=pl.BlockSpec(memory_space=pl.ANY),
        out_shape=jax.ShapeDtypeStruct((order.shape[0], 2 * TILE, RADIX), BF16),
        scratch_shapes=[pltpu.VMEM((BUFFERS, TILES_SLOTS, 2 * TILE, RADIX), BF16), pltpu.SemaphoreType.DMA((BUFFERS,))],
        compiler_params=pltpu.CompilerParams(vmem_limit_bytes=36 * MIB),
        cost_estimate=pl.CostEstimate(flops=order.shape[0] * RADIX ** 3 * 8, bytes_accessed=64 * MIB, transcendentals=0),
        name="tiles",
    )(order, row, block, steps, table, spectrum)


def copies(scalars, packed_ref, v_ref, u_ref, sems, step, buffer):
    order_ref, window_ref, half_ref = scalars
    started = []
    for i in range(STEP_SLOTS):
        slot = order_ref[step * STEP_SLOTS + i]
        window = window_ref[slot]
        half = half_ref[slot]
        from_row = pl.multiple_of(half * TILE, TILE)
        started.append(pltpu.make_async_copy(packed_ref.at[pl.ds(window, 2), :TILE], v_ref.at[buffer, i], sems.at[buffer, i, 0]))
        started.append(pltpu.make_async_copy(packed_ref.at[pl.ds(window, 2), TILE:], u_ref.at[buffer, i, half, :, pl.ds(from_row, TILE)], sems.at[buffer, i, 1]))
    return started


def over_steps(steps, fetch, work):
    ahead = BUFFERS - 1
    for step in range(ahead):
        for copy in fetch(step, step):
            copy.start()

    def step_body(step, _):
        buffer = lax.rem(step, BUFFERS)

        @pl.when(step + ahead < steps)
        def _():
            for copy in fetch(step + ahead, lax.rem(step + ahead, BUFFERS)):
                copy.start()

        for copy in fetch(step, buffer):
            copy.wait()
        work(step, buffer)
        return 0

    lax.fori_loop(0, steps, step_body, 0)


def clear_sides(u_ref):
    for buffer in range(BUFFERS):
        for i in range(STEP_SLOTS):
            u_ref[buffer, i] = jnp.zeros(u_ref.shape[2:], BF16)


def side_by_side(pair):
    return jnp.concatenate([pair[0], pair[1]], axis=1)


def model_kernel(resident, order_ref, window_ref, low_ref, high_ref, half_ref, steps_ref, packed_ref, tiles_ref, out_ref, t_ref, t_sems, *buffers):
    column = lax.broadcasted_iota(jnp.int32, (1, 2 * VIS_SLOT), 1)
    if not resident:
        v_ref, u_ref, sems = buffers
        clear_sides(u_ref)

    def fetch(step, buffer):
        started = [pltpu.make_async_copy(tiles_ref.at[pl.ds(step * STEP_SLOTS, STEP_SLOTS)], t_ref.at[buffer], t_sems.at[buffer])]
        if not resident:
            started += copies((order_ref, window_ref, half_ref), packed_ref, v_ref, u_ref, sems, step, buffer)
        return started

    def weights(i, slot, buffer):
        if not resident:
            return side_by_side(v_ref[buffer, i]), side_by_side(u_ref[buffer, i, half_ref[slot]])
        window = window_ref[slot]
        along_v = side_by_side([packed_ref[window, :TILE], packed_ref[window + 1, :TILE]])
        along_u = side_by_side([packed_ref[window, TILE:], packed_ref[window + 1, TILE:]])
        none = jnp.zeros_like(along_u)
        upper = half_ref[slot] == 1
        return along_v, jnp.concatenate([jnp.where(upper, none, along_u), jnp.where(upper, along_u, none)], axis=0)

    def work(step, buffer):
        found = []
        for i in range(STEP_SLOTS):
            slot = order_ref[step * STEP_SLOTS + i]
            weights_v, weights_u = weights(i, slot, buffer)
            inner = dot(t_ref[buffer, i], weights_u)
            weights_v = weights_v.astype(F32)
            real = jnp.sum(inner[:TILE] * weights_v, axis=0, keepdims=True)
            imag = jnp.sum(inner[TILE:] * weights_v, axis=0, keepdims=True)
            mine = (column >= low_ref[slot]) & (column < high_ref[slot])
            found.append((window_ref[slot], mine, jnp.concatenate([real, imag], axis=0)))
        for window, mine, both in found:
            out_ref[window] = jnp.where(mine[:, :VIS_SLOT], both[:, :VIS_SLOT], out_ref[window])
            out_ref[window + 1] = jnp.where(mine[:, VIS_SLOT:], both[:, VIS_SLOT:], out_ref[window + 1])

    over_steps(steps_ref[0], fetch, work)


def slot_buffers():
    return [
        pltpu.VMEM((BUFFERS, STEP_SLOTS, 2, TILE, VIS_SLOT), BF16),
        pltpu.VMEM((BUFFERS, STEP_SLOTS, 2, 2, 2 * TILE, VIS_SLOT), BF16),
    ]


def model_parts(scalars, packed, tiles):
    order, window, low, high, row, half, block, steps = scalars
    resident = packed.size * 2 <= RESIDENT_BYTES
    buffers = [] if resident else slot_buffers() + [pltpu.SemaphoreType.DMA((BUFFERS, STEP_SLOTS, 2))]
    return pl.pallas_call(
        functools.partial(model_kernel, resident),
        in_specs=[pl.BlockSpec(memory_space=pltpu.SMEM)] * 6 + [pl.BlockSpec(memory_space=pltpu.VMEM if resident else pl.ANY), pl.BlockSpec(memory_space=pl.ANY)],
        out_specs=pl.BlockSpec(memory_space=pltpu.VMEM),
        out_shape=jax.ShapeDtypeStruct((packed.shape[0], 2, VIS_SLOT), F32),
        scratch_shapes=[pltpu.VMEM((BUFFERS, STEP_SLOTS, 2 * TILE, RADIX), BF16), pltpu.SemaphoreType.DMA((BUFFERS,))] + buffers,
        compiler_params=pltpu.CompilerParams(vmem_limit_bytes=40 * MIB),
        cost_estimate=pl.CostEstimate(flops=order.shape[0] * RADIX ** 3 * 4, bytes_accessed=96 * MIB, transcendentals=0),
        name="model",
    )(order, window, low, high, half, steps, packed, tiles)


def gradient_kernel(order_ref, window_ref, low_ref, high_ref, row_ref, half_ref, block_ref, steps_ref, table_ref, residual_ref, packed_ref, out_ref, total, v_ref, u_ref, sems):
    column = lax.broadcasted_iota(jnp.int32, (1, 2 * VIS_SLOT), 1)
    clear_sides(u_ref)

    def clear(j, _):
        total[j] = jnp.zeros(total.shape[1:], F32)
        return 0

    lax.fori_loop(0, HALF_BLOCKS, clear, 0)

    def fetch(step, buffer):
        return copies((order_ref, window_ref, half_ref), packed_ref, v_ref, u_ref, sems, step, buffer)

    def work(step, buffer):
        found = []
        for pair in range(STEP_PAIRS):
            slots = [order_ref[step * STEP_SLOTS + 2 * pair + i] for i in range(2)]
            tiles = []
            for i, slot in enumerate(slots):
                at = 2 * pair + i
                window = window_ref[slot]
                mine = (column >= low_ref[slot]) & (column < high_ref[slot])
                residual = side_by_side([residual_ref[window], residual_ref[window + 1]])
                residual = jnp.where(mine, residual, 0.0)
                weights_v = side_by_side(v_ref[buffer, at]).astype(F32)
                weighted = jnp.concatenate([weights_v * residual[0:1], weights_v * residual[1:2]], axis=0).astype(BF16)
                tile = dot_nt(weighted, side_by_side(u_ref[buffer, at, half_ref[slot]]))
                real, imag = tile[:TILE], tile[TILE:]
                tiles.append(jnp.concatenate([real, imag], axis=1))
                tiles.append(jnp.concatenate([-imag, real], axis=1))
            found.append((slots, jnp.concatenate(tiles, axis=0).astype(BF16)))
        for pair, (slots, both) in enumerate(found):
            tables = jnp.concatenate([table_ref[row_ref[slot]] for slot in slots], axis=1)
            block = block_ref[step * STEP_PAIRS + pair]
            total[block] = total[block] + dot(tables, both)

    over_steps(steps_ref[0], fetch, work)

    def round_off(j, _):
        out_ref[j] = total[j].astype(BF16)
        return 0

    lax.fori_loop(0, HALF_BLOCKS, round_off, 0)


def gradient_columns(scalars, table, residual, packed, rows):
    return pl.pallas_call(
        gradient_kernel,
        in_specs=[pl.BlockSpec(memory_space=pltpu.SMEM)] * 8 + [pl.BlockSpec(memory_space=pltpu.VMEM)] * 2 + [pl.BlockSpec(memory_space=pl.ANY)],
        out_specs=pl.BlockSpec(memory_space=pltpu.VMEM),
        out_shape=jax.ShapeDtypeStruct((HALF_BLOCKS, rows, 2 * RADIX), BF16),
        scratch_shapes=[pltpu.VMEM((HALF_BLOCKS, rows, 2 * RADIX), F32)] + slot_buffers() + [pltpu.SemaphoreType.DMA((BUFFERS, STEP_SLOTS, 2))],
        compiler_params=pltpu.CompilerParams(vmem_limit_bytes=56 * MIB),
        cost_estimate=pl.CostEstimate(flops=scalars[0].shape[0] * RADIX ** 3 * 8, bytes_accessed=96 * MIB, transcendentals=0),
        name="gradient",
    )(*scalars, table, residual, packed)


def column_tables(first_row, rows):
    y = first_row + jnp.arange(rows, dtype=jnp.int32)
    r = jnp.arange(TILE_ROWS, dtype=jnp.int32)
    a = jnp.arange(TILE, dtype=jnp.int32)
    coarse = (r[:, None] * y[None, :] % TILE_ROWS).astype(F32) * (2.0 * math.pi / TILE_ROWS)
    fine = (a[:, None] * y[None, :] % SIDE).astype(F32) * (2.0 * math.pi / SIDE)
    coarse_cos, coarse_sin = jnp.cos(coarse), jnp.sin(coarse)
    fine_cos, fine_sin = jnp.cos(fine) / RADIX, jnp.sin(fine) / RADIX
    with_cos = jnp.concatenate([fine_cos, fine_sin])
    with_sin = jnp.concatenate([fine_sin, -fine_cos])
    forward = coarse_cos[:, None, :] * with_cos[None] - coarse_sin[:, None, :] * with_sin[None]
    inverse = coarse_cos[:, :, None] * with_cos.T[None] - coarse_sin[:, :, None] * with_sin.T[None]
    return forward.astype(BF16), inverse.astype(BF16)


def firsts(counts):
    slot = jnp.arange(counts.shape[1], dtype=jnp.int32)
    ahead = slot[None, None, :] < slot[None, :, None]
    return jnp.sum(jnp.where(ahead, counts[:, None, :], 0), axis=2)


def spread(values, band_count):
    return lax.all_to_all(jnp.broadcast_to(values[None], (band_count,) + values.shape), "band", 0, 0, tiled=True)


def on_device(sky_image, tile_band, tile_place, counts, kernel, observed):
    band_count = lax.axis_size("band")
    rows = sky_image.shape[0]
    slots_here = tile_place.shape[0]
    slots_all = band_count * slots_here
    tiles_across = sky_image.shape[1] // 2 // band_count // TILE
    tiles_here = slots_here // 2

    tile_row = tile_place // tiles_across
    tile_col = tile_band[:, 0] * tiles_across + tile_place % tiles_across
    seen = jnp.pad(observed.astype(F32), ((0, 0), (0, 6), (0, 0)))
    packed, seen = pack(firsts(counts)[0], kernel, seen, tiles_here)
    seen = seen[:tiles_here, :2]
    packed = lax.all_gather(packed, "band", tiled=True)

    every = spread(jnp.stack([tile_row, tile_col, counts[0]]), band_count)
    all_row, all_col = (every[:, i].reshape(slots_all) for i in range(2))
    all_block = all_col // 2
    all_first = firsts(every[:, 2])
    all_window = jnp.minimum(all_first // VIS_SLOT, tiles_here - 2)
    all_low = all_first - all_window * VIS_SLOT
    all_high = (all_low + every[:, 2]).reshape(slots_all)
    all_low = all_low.reshape(slots_all)
    all_window = (all_window + tiles_here * jnp.arange(band_count, dtype=jnp.int32)[:, None]).reshape(slots_all)

    spectrum = rows_forward(sky_image)
    forward_table, inverse_table = column_tables(lax.axis_index("band").astype(jnp.int32) * rows, rows)

    slot = jnp.arange(slots_all, dtype=jnp.int32)
    block = jnp.arange(HALF_BLOCKS, dtype=jnp.int32)
    in_block = jnp.sum((all_block[:, None] == block[None, :]).astype(jnp.int32), axis=0)
    pairs_of = (in_block + 1) // 2
    pairs_to = jnp.sum(jnp.where(block[None, :] <= block[:, None], pairs_of[None, :], 0), axis=1)
    rank = jnp.sum(((all_block[:, None] == all_block[None, :]) & (slot[None, :] < slot[:, None])).astype(jnp.int32), axis=1)
    first_pair = jnp.sum(jnp.where(block[None, :] < all_block[:, None], pairs_of[None, :], 0), axis=1)
    position = 2 * first_pair + rank
    positions_most = (slots_all + HALF_BLOCKS + TILES_SLOTS - 1) // TILES_SLOTS * TILES_SLOTS
    positions = jnp.arange(positions_most, dtype=jnp.int32)
    order = slots_all + jnp.sum(jnp.where(position[None, :] == positions[:, None], slot[None, :] - slots_all, 0), axis=1)
    pair_block = jnp.sum((pairs_to[None, :] <= positions[:positions_most // 2, None]).astype(jnp.int32), axis=1)
    pair_block = jnp.minimum(pair_block, HALF_BLOCKS - 1)
    steps = (pairs_to[-1:] + STEP_PAIRS - 1) // STEP_PAIRS

    def spare(values):
        return jnp.pad(values, (0, 8))

    scalars = (order, spare(all_window), spare(all_low), spare(all_high), spare(all_row), spare(all_col % 2), pair_block, steps)
    tiles = tile_parts(scalars, forward_table, spectrum)
    parts = model_parts(scalars, packed, tiles).reshape(band_count, tiles_here, 2, VIS_SLOT)
    residual = seen - jnp.sum(lax.all_to_all(parts, "band", 0, 0, tiled=True), axis=0)
    residual = spread(residual, band_count).reshape(band_count * tiles_here, 2, VIS_SLOT)
    columns = gradient_columns(scalars, inverse_table, residual, packed, rows)
    return rows_inverse(columns)


def solution(mesh):
    return jax.shard_map(
        on_device,
        mesh=mesh,
        in_specs=(
            P(("parts", "band"), None),
            P(("parts", "band"), None),
            P(("parts", "band")),
            P(("parts", "band"), None),
            P(("parts", "band"), None, None),
            P(("parts", "band"), None, None),
        ),
        out_specs=P(("parts", "band"), None),
        check_vma=False,
    )
```

```python
import functools
import math

import jax
import jax.numpy as jnp
import numpy as np
from jax import lax
from jax.experimental import pallas as pl
from jax.experimental.pallas import tpu as pltpu
from jax.sharding import PartitionSpec as P

RADIX = 128
SIDE = RADIX * RADIX
TILE = 64
HALF_BLOCKS = RADIX // 2
TILE_ROWS = SIDE // TILE
VIS_SLOT = 128
ROW_PITCH = RADIX + 8
ROWS_STEP = 16
STEP_PAIRS = 8
STEP_SLOTS = 2 * STEP_PAIRS
BUFFERS = 4
TILES_PAIRS = 16
TILES_SLOTS = 2 * TILES_PAIRS
RESIDENT_BYTES = 16 << 20
F32 = jnp.float32
BF16 = jnp.bfloat16
NT = (((1,), (1,)), ((), ()))
MIB = 1 << 20


def dot(a, b):
    return jnp.dot(a, b, preferred_element_type=F32)


def dot_nt(a, b):
    return lax.dot_general(a, b, NT, preferred_element_type=F32)


def radix_tables():
    index = np.arange(RADIX)
    angle = (index[:, None] * index[None, :] % RADIX) * (2.0 * math.pi / RADIX)
    turn = (index[:, None] * index[None, :]) * (2.0 * math.pi / SIDE)
    twist = np.concatenate([np.cos(turn), np.sin(turn)]) / RADIX
    return np.cos(angle), np.sin(angle), twist.astype(np.float32)


def whole(shape, space=pltpu.VMEM):
    return pl.BlockSpec(shape, lambda *_: (0,) * len(shape), memory_space=space)


def two_by_two(apart, head_ref, tail_ref, done, twisted):
    def two_rows(i, _):
        first = apart[pl.ds(pl.multiple_of(2 * i * ROW_PITCH, 8), RADIX), :]
        second = apart[pl.ds(pl.multiple_of((2 * i + 1) * ROW_PITCH, 8), RADIX), :]
        mixed = dot(head_ref[...], jnp.concatenate([first, second], axis=1).astype(BF16))
        for side in range(2):
            part = slice(side * RADIX, (side + 1) * RADIX)
            middle = jnp.concatenate(twisted(mixed[:RADIX, part], mixed[RADIX:, part]), axis=1).astype(BF16)
            done[pl.ds(pl.multiple_of((2 * i + side) * ROW_PITCH, 8), RADIX), :] = dot_nt(tail_ref[...], middle)
        return 0

    lax.fori_loop(0, ROWS_STEP // 2, two_rows, 0, unroll=True)


def rows_forward_kernel(sky_ref, head_ref, twist_ref, tail_ref, out_ref, apart, done):
    for a in range(RADIX):
        apart[pl.ds(a, ROWS_STEP, stride=ROW_PITCH), :] = sky_ref[:, a * RADIX:(a + 1) * RADIX].astype(F32)

    def twisted(by_cos, by_sin):
        twist_cos, twist_sin = twist_ref[:RADIX], twist_ref[RADIX:]
        return [by_cos * twist_cos - by_sin * twist_sin, -(by_cos * twist_sin + by_sin * twist_cos)]

    two_by_two(apart, head_ref, tail_ref, done, twisted)
    for j in range(HALF_BLOCKS):
        real = done[pl.ds(j, ROWS_STEP, stride=ROW_PITCH), :]
        imag = done[pl.ds(HALF_BLOCKS + j, ROWS_STEP, stride=ROW_PITCH), :]
        out_ref[j] = jnp.concatenate([real, imag], axis=1).astype(BF16)


def rows_forward(sky):
    rows = sky.shape[0]
    cos, sin, twist = radix_tables()
    head = jnp.asarray(np.concatenate([cos, sin]), BF16)
    tail = jnp.asarray(np.block([[cos[:HALF_BLOCKS], sin[:HALF_BLOCKS]], [-sin[:HALF_BLOCKS], cos[:HALF_BLOCKS]]]), BF16)
    return pl.pallas_call(
        rows_forward_kernel,
        grid=(rows // ROWS_STEP,),
        in_specs=[pl.BlockSpec((ROWS_STEP, SIDE), lambda i: (i, 0)), whole(head.shape), whole(twist.shape), whole(tail.shape)],
        out_specs=pl.BlockSpec((HALF_BLOCKS, ROWS_STEP, 2 * RADIX), lambda i: (0, i, 0)),
        out_shape=jax.ShapeDtypeStruct((HALF_BLOCKS, rows, 2 * RADIX), BF16),
        scratch_shapes=[pltpu.VMEM((ROWS_STEP * ROW_PITCH, RADIX), F32), pltpu.VMEM((ROWS_STEP * ROW_PITCH, RADIX), F32)],
        compiler_params=pltpu.CompilerParams(vmem_limit_bytes=24 * MIB),
        cost_estimate=pl.CostEstimate(flops=rows * RADIX * RADIX * 1024, bytes_accessed=rows * SIDE * 4, transcendentals=0),
        name="rows_forward",
    )(sky, head, jnp.asarray(twist), tail)


def rows_inverse(total, head_ref, twist_ref, tail_ref, out_ref, apart, done, lines, line_sems):
    blocks = out_ref.shape[0] // ROWS_STEP

    def twisted(real, imag):
        twist_cos, twist_sin = twist_ref[:RADIX], twist_ref[RADIX:]
        return [real * twist_cos - imag * twist_sin, real * twist_sin + imag * twist_cos]

    def leave(i):
        buffer = lax.rem(i, 2)
        return pltpu.make_async_copy(lines.at[buffer], out_ref.at[pl.ds(pl.multiple_of(i * ROWS_STEP, ROWS_STEP), ROWS_STEP)], line_sems.at[buffer])

    def one_block(i, _):
        buffer = lax.rem(i, 2)
        rows = pl.ds(pl.multiple_of(i * ROWS_STEP, ROWS_STEP), ROWS_STEP)
        for j in range(HALF_BLOCKS):
            apart[pl.ds(j, ROWS_STEP, stride=ROW_PITCH), :] = total[j, rows, :RADIX]
            apart[pl.ds(HALF_BLOCKS + j, ROWS_STEP, stride=ROW_PITCH), :] = total[j, rows, RADIX:]
        two_by_two(apart, head_ref, tail_ref, done, twisted)

        @pl.when(i >= 2)
        def _():
            leave(i - 2).wait()

        for j in range(RADIX):
            lines[buffer, :, j * RADIX:(j + 1) * RADIX] = done[pl.ds(j, ROWS_STEP, stride=ROW_PITCH), :].astype(BF16)
        leave(i).start()
        return 0

    lax.fori_loop(0, blocks, one_block, 0)
    for back in range(min(2, blocks), 0, -1):
        leave(blocks - back).wait()


def inverse_tables():
    cos, sin, twist = radix_tables()
    used_cos, used_sin = cos[:, :HALF_BLOCKS], sin[:, :HALF_BLOCKS]
    head = np.block([[used_cos, -used_sin], [used_sin, used_cos]])
    tail = np.concatenate([cos, -sin], axis=1)
    return jnp.asarray(head, BF16), jnp.asarray(twist), jnp.asarray(tail, BF16)


def pack_kernel(first_ref, weights_ref, out_ref, lined):
    def one(slot, _):
        lined[pl.ds(first_ref[slot], VIS_SLOT), :] = weights_ref[slot].astype(F32)
        return 0

    lax.fori_loop(0, weights_ref.shape[0], one, 0, unroll=4)
    for tile in range(out_ref.shape[0]):
        out_ref[tile] = lined[tile * VIS_SLOT:(tile + 1) * VIS_SLOT, :].T.astype(BF16)


def pack(first, weights, tiles):
    return pl.pallas_call(
        pack_kernel,
        in_specs=[pl.BlockSpec(memory_space=pltpu.SMEM), pl.BlockSpec(memory_space=pltpu.VMEM)],
        out_specs=pl.BlockSpec(memory_space=pltpu.VMEM),
        out_shape=jax.ShapeDtypeStruct((tiles, 2 * TILE, VIS_SLOT), BF16),
        scratch_shapes=[pltpu.VMEM(((tiles + 1) * VIS_SLOT, 2 * TILE), F32)],
        compiler_params=pltpu.CompilerParams(vmem_limit_bytes=16 * MIB),
        cost_estimate=pl.CostEstimate(flops=0, bytes_accessed=4 * MIB, transcendentals=0),
        name="pack",
    )(first, weights)


def line_up_kernel(first_ref, observed_ref, seen_ref):
    column = lax.broadcasted_iota(jnp.int32, (8, VIS_SLOT), 1)

    def one(slot, _):
        tile, shift = first_ref[slot] // VIS_SLOT, first_ref[slot] % VIS_SLOT
        turned = pltpu.roll(observed_ref[slot], shift, 1)
        seen_ref[tile] = jnp.where(column >= shift, turned, seen_ref[tile])
        seen_ref[tile + 1] = turned
        return 0

    lax.fori_loop(0, observed_ref.shape[0], one, 0)


def line_up(first, observed, tiles):
    padded = jnp.pad(observed.astype(F32), ((0, 0), (0, 6), (0, 0)))
    seen = pl.pallas_call(
        line_up_kernel,
        in_specs=[pl.BlockSpec(memory_space=pltpu.SMEM), pl.BlockSpec(memory_space=pltpu.VMEM)],
        out_specs=pl.BlockSpec(memory_space=pltpu.VMEM),
        out_shape=jax.ShapeDtypeStruct((tiles + 1, 8, VIS_SLOT), F32),
        name="line_up",
    )(first, padded)
    return seen[:tiles, :2]


def tiles_kernel(order_ref, row_ref, block_ref, steps_ref, table_ref, spectrum_ref, out_ref, ready, sems):
    steps = (steps_ref[0] * STEP_PAIRS + TILES_PAIRS - 1) // TILES_PAIRS

    def leave(step, buffer):
        return pltpu.make_async_copy(ready.at[buffer], out_ref.at[pl.ds(step * TILES_SLOTS, TILES_SLOTS)], sems.at[buffer])

    def step_body(step, _):
        buffer = lax.rem(step, BUFFERS)

        @pl.when(step >= BUFFERS)
        def _():
            leave(step - BUFFERS, buffer).wait()

        for pair in range(TILES_PAIRS):
            slots = [order_ref[step * TILES_SLOTS + 2 * pair + i] for i in range(2)]
            columns = spectrum_ref[block_ref[step * TILES_PAIRS + pair]]
            tables = jnp.concatenate([table_ref[row_ref[slot]] for slot in slots], axis=0)
            turned = dot(tables, columns)
            for i in range(2):
                base = 2 * TILE * i
                by_cos, by_sin = turned[base:base + TILE], turned[base + TILE:base + 2 * TILE]
                ready[buffer, 2 * pair + i, :TILE] = (by_cos[:, :RADIX] + by_sin[:, RADIX:]).astype(BF16)
                ready[buffer, 2 * pair + i, TILE:] = (by_cos[:, RADIX:] - by_sin[:, :RADIX]).astype(BF16)
        leave(step, buffer).start()
        return 0

    lax.fori_loop(0, steps, step_body, 0)
    for back in range(BUFFERS, 0, -1):
        leave(steps - back, lax.rem(steps - back, BUFFERS)).wait()


def tile_parts(scalars, table, spectrum):
    order, window, low, high, row, half, block, steps = scalars
    return pl.pallas_call(
        tiles_kernel,
        in_specs=[pl.BlockSpec(memory_space=pltpu.SMEM)] * 4 + [pl.BlockSpec(memory_space=pltpu.VMEM)] * 2,
        out_specs=pl.BlockSpec(memory_space=pl.ANY),
        out_shape=jax.ShapeDtypeStruct((order.shape[0], 2 * TILE, RADIX), BF16),
        scratch_shapes=[pltpu.VMEM((BUFFERS, TILES_SLOTS, 2 * TILE, RADIX), BF16), pltpu.SemaphoreType.DMA((BUFFERS,))],
        compiler_params=pltpu.CompilerParams(vmem_limit_bytes=30 * MIB),
        cost_estimate=pl.CostEstimate(flops=order.shape[0] * RADIX ** 3 * 8, bytes_accessed=64 * MIB, transcendentals=0),
        name="tiles",
    )(order, row, block, steps, table, spectrum)


def copies(scalars, packed_ref, v_ref, u_ref, sems, step, buffer):
    order_ref, window_ref, half_ref = scalars
    started = []
    for i in range(STEP_SLOTS):
        slot = order_ref[step * STEP_SLOTS + i]
        window = window_ref[slot]
        half = half_ref[slot]
        from_row = pl.multiple_of(half * TILE, TILE)
        started.append(pltpu.make_async_copy(packed_ref.at[pl.ds(window, 2), :TILE], v_ref.at[buffer, i], sems.at[buffer, i, 0]))
        started.append(pltpu.make_async_copy(packed_ref.at[pl.ds(window, 2), TILE:], u_ref.at[buffer, i, half, :, pl.ds(from_row, TILE)], sems.at[buffer, i, 1]))
    return started


def over_steps(steps, fetch, work):
    ahead = BUFFERS - 1
    for step in range(ahead):
        for copy in fetch(step, step):
            copy.start()

    def step_body(step, _):
        buffer = lax.rem(step, BUFFERS)

        @pl.when(step + ahead < steps)
        def _():
            for copy in fetch(step + ahead, lax.rem(step + ahead, BUFFERS)):
                copy.start()

        for copy in fetch(step, buffer):
            copy.wait()
        work(step, buffer)
        return 0

    lax.fori_loop(0, steps, step_body, 0)


def clear_sides(u_ref):
    for buffer in range(BUFFERS):
        for i in range(STEP_SLOTS):
            u_ref[buffer, i] = jnp.zeros(u_ref.shape[2:], BF16)


def side_by_side(pair):
    return jnp.concatenate([pair[0], pair[1]], axis=1)


def model_kernel(resident, order_ref, window_ref, low_ref, high_ref, half_ref, steps_ref, packed_ref, tiles_ref, out_ref, t_ref, t_sems, *buffers):
    column = lax.broadcasted_iota(jnp.int32, (1, 2 * VIS_SLOT), 1)
    if not resident:
        v_ref, u_ref, sems = buffers
        clear_sides(u_ref)

    def fetch(step, buffer):
        started = [pltpu.make_async_copy(tiles_ref.at[pl.ds(step * STEP_SLOTS, STEP_SLOTS)], t_ref.at[buffer], t_sems.at[buffer])]
        if not resident:
            started += copies((order_ref, window_ref, half_ref), packed_ref, v_ref, u_ref, sems, step, buffer)
        return started

    def weights(i, slot, buffer):
        if not resident:
            return side_by_side(v_ref[buffer, i]), side_by_side(u_ref[buffer, i, half_ref[slot]])
        window = window_ref[slot]
        along_v = side_by_side([packed_ref[window, :TILE], packed_ref[window + 1, :TILE]])
        along_u = side_by_side([packed_ref[window, TILE:], packed_ref[window + 1, TILE:]])
        none = jnp.zeros_like(along_u)
        upper = half_ref[slot] == 1
        return along_v, jnp.concatenate([jnp.where(upper, none, along_u), jnp.where(upper, along_u, none)], axis=0)

    def work(step, buffer):
        found = []
        for i in range(STEP_SLOTS):
            slot = order_ref[step * STEP_SLOTS + i]
            weights_v, weights_u = weights(i, slot, buffer)
            inner = dot(t_ref[buffer, i], weights_u)
            weights_v = weights_v.astype(F32)
            real = jnp.sum(inner[:TILE] * weights_v, axis=0, keepdims=True)
            imag = jnp.sum(inner[TILE:] * weights_v, axis=0, keepdims=True)
            mine = (column >= low_ref[slot]) & (column < high_ref[slot])
            found.append((window_ref[slot], mine, jnp.concatenate([real, imag], axis=0)))
        for window, mine, both in found:
            out_ref[window] = jnp.where(mine[:, :VIS_SLOT], both[:, :VIS_SLOT], out_ref[window])
            out_ref[window + 1] = jnp.where(mine[:, VIS_SLOT:], both[:, VIS_SLOT:], out_ref[window + 1])

    over_steps(steps_ref[0], fetch, work)


def slot_buffers():
    return [
        pltpu.VMEM((BUFFERS, STEP_SLOTS, 2, TILE, VIS_SLOT), BF16),
        pltpu.VMEM((BUFFERS, STEP_SLOTS, 2, 2, 2 * TILE, VIS_SLOT), BF16),
    ]


def model_parts(scalars, packed, tiles):
    order, window, low, high, row, half, block, steps = scalars
    resident = packed.size * 2 <= RESIDENT_BYTES
    buffers = [] if resident else slot_buffers() + [pltpu.SemaphoreType.DMA((BUFFERS, STEP_SLOTS, 2))]
    return pl.pallas_call(
        functools.partial(model_kernel, resident),
        in_specs=[pl.BlockSpec(memory_space=pltpu.SMEM)] * 6 + [pl.BlockSpec(memory_space=pltpu.VMEM if resident else pl.ANY), pl.BlockSpec(memory_space=pl.ANY)],
        out_specs=pl.BlockSpec(memory_space=pltpu.VMEM),
        out_shape=jax.ShapeDtypeStruct((packed.shape[0], 2, VIS_SLOT), F32),
        scratch_shapes=[pltpu.VMEM((BUFFERS, STEP_SLOTS, 2 * TILE, RADIX), BF16), pltpu.SemaphoreType.DMA((BUFFERS,))] + buffers,
        compiler_params=pltpu.CompilerParams(vmem_limit_bytes=22 * MIB),
        cost_estimate=pl.CostEstimate(flops=order.shape[0] * RADIX ** 3 * 4, bytes_accessed=96 * MIB, transcendentals=0),
        name="model",
    )(order, window, low, high, half, steps, packed, tiles)


def gradient_kernel(order_ref, window_ref, low_ref, high_ref, row_ref, half_ref, block_ref, steps_ref, table_ref, residual_ref, head_ref, twist_ref, tail_ref, packed_ref, out_ref, total, v_ref, u_ref, sems, *lines):
    column = lax.broadcasted_iota(jnp.int32, (1, 2 * VIS_SLOT), 1)
    clear_sides(u_ref)

    def clear(j, _):
        total[j] = jnp.zeros(total.shape[1:], F32)
        return 0

    lax.fori_loop(0, HALF_BLOCKS, clear, 0)

    def fetch(step, buffer):
        return copies((order_ref, window_ref, half_ref), packed_ref, v_ref, u_ref, sems, step, buffer)

    def work(step, buffer):
        found = []
        for pair in range(STEP_PAIRS):
            slots = [order_ref[step * STEP_SLOTS + 2 * pair + i] for i in range(2)]
            tiles = []
            for i, slot in enumerate(slots):
                at = 2 * pair + i
                window = window_ref[slot]
                mine = (column >= low_ref[slot]) & (column < high_ref[slot])
                residual = side_by_side([residual_ref[window], residual_ref[window + 1]])
                residual = jnp.where(mine, residual, 0.0)
                weights_v = side_by_side(v_ref[buffer, at]).astype(F32)
                weighted = jnp.concatenate([weights_v * residual[0:1], weights_v * residual[1:2]], axis=0).astype(BF16)
                tile = dot_nt(weighted, side_by_side(u_ref[buffer, at, half_ref[slot]]))
                real, imag = tile[:TILE], tile[TILE:]
                tiles.append(jnp.concatenate([real, imag], axis=1))
                tiles.append(jnp.concatenate([-imag, real], axis=1))
            found.append((slots, jnp.concatenate(tiles, axis=0).astype(BF16)))
        for pair, (slots, both) in enumerate(found):
            tables = jnp.concatenate([table_ref[row_ref[slot]] for slot in slots], axis=1)
            block = block_ref[step * STEP_PAIRS + pair]
            total[block] = total[block] + dot(tables, both)

    over_steps(steps_ref[0], fetch, work)

    rows_inverse(total, head_ref, twist_ref, tail_ref, out_ref, *lines)


def gradient_rows(scalars, table, residual, packed, rows):
    return pl.pallas_call(
        gradient_kernel,
        in_specs=[pl.BlockSpec(memory_space=pltpu.SMEM)] * 8 + [pl.BlockSpec(memory_space=pltpu.VMEM)] * 5 + [pl.BlockSpec(memory_space=pl.ANY)],
        out_specs=pl.BlockSpec(memory_space=pl.ANY),
        out_shape=jax.ShapeDtypeStruct((rows, SIDE), BF16),
        scratch_shapes=[pltpu.VMEM((HALF_BLOCKS, rows, 2 * RADIX), F32)] + slot_buffers() + [
            pltpu.SemaphoreType.DMA((BUFFERS, STEP_SLOTS, 2)),
            pltpu.VMEM((ROWS_STEP * ROW_PITCH, RADIX), F32),
            pltpu.VMEM((ROWS_STEP * ROW_PITCH, RADIX), F32),
            pltpu.VMEM((2, ROWS_STEP, SIDE), BF16),
            pltpu.SemaphoreType.DMA((2,)),
        ],
        compiler_params=pltpu.CompilerParams(vmem_limit_bytes=47 * MIB),
        cost_estimate=pl.CostEstimate(flops=scalars[0].shape[0] * RADIX ** 3 * 8, bytes_accessed=96 * MIB, transcendentals=0),
        name="gradient",
    )(*scalars, table, residual, *inverse_tables(), packed)


def column_tables(first_row, rows):
    y = first_row + jnp.arange(rows, dtype=jnp.int32)
    r = jnp.arange(TILE_ROWS, dtype=jnp.int32)
    a = jnp.arange(TILE, dtype=jnp.int32)
    coarse = (r[:, None] * y[None, :] % TILE_ROWS).astype(F32) * (2.0 * math.pi / TILE_ROWS)
    fine = (a[:, None] * y[None, :] % SIDE).astype(F32) * (2.0 * math.pi / SIDE)
    coarse_cos, coarse_sin = jnp.cos(coarse), jnp.sin(coarse)
    fine_cos, fine_sin = jnp.cos(fine) / RADIX, jnp.sin(fine) / RADIX
    with_cos = jnp.concatenate([fine_cos, fine_sin])
    with_sin = jnp.concatenate([fine_sin, -fine_cos])
    forward = coarse_cos[:, None, :] * with_cos[None] - coarse_sin[:, None, :] * with_sin[None]
    inverse = coarse_cos[:, :, None] * with_cos.T[None] - coarse_sin[:, :, None] * with_sin.T[None]
    return lax.optimization_barrier((forward.astype(BF16), inverse.astype(BF16)))


def firsts(counts):
    slot = jnp.arange(counts.shape[1], dtype=jnp.int32)
    ahead = slot[None, None, :] < slot[None, :, None]
    return jnp.sum(jnp.where(ahead, counts[:, None, :], 0), axis=2)


def spread(values, band_count):
    return lax.all_to_all(jnp.broadcast_to(values[None], (band_count,) + values.shape), "band", 0, 0, tiled=True)


def on_device(sky_image, tile_band, tile_place, counts, kernel, observed):
    band_count = lax.axis_size("band")
    rows = sky_image.shape[0]
    slots_here = tile_place.shape[0]
    slots_all = band_count * slots_here
    tiles_across = sky_image.shape[1] // 2 // band_count // TILE
    tiles_here = slots_here // 2

    tile_row = tile_place // tiles_across
    tile_col = tile_band[:, 0] * tiles_across + tile_place % tiles_across
    first = firsts(counts)[0]
    packed = lax.all_gather(pack(first, kernel, tiles_here), "band", tiled=True)
    seen = line_up(first, observed, tiles_here)

    every = spread(jnp.stack([tile_row, tile_col, counts[0]]), band_count)
    all_row, all_col = (every[:, i].reshape(slots_all) for i in range(2))
    all_block = all_col // 2
    all_first = firsts(every[:, 2])
    all_window = jnp.minimum(all_first // VIS_SLOT, tiles_here - 2)
    all_low = all_first - all_window * VIS_SLOT
    all_high = (all_low + every[:, 2]).reshape(slots_all)
    all_low = all_low.reshape(slots_all)
    all_window = (all_window + tiles_here * jnp.arange(band_count, dtype=jnp.int32)[:, None]).reshape(slots_all)

    spectrum = rows_forward(sky_image)
    forward_table, inverse_table = column_tables(lax.axis_index("band").astype(jnp.int32) * rows, rows)

    slot = jnp.arange(slots_all, dtype=jnp.int32)
    block = jnp.arange(HALF_BLOCKS, dtype=jnp.int32)
    in_block = jnp.sum((all_block[:, None] == block[None, :]).astype(jnp.int32), axis=0)
    pairs_of = (in_block + 1) // 2
    pairs_to = jnp.sum(jnp.where(block[None, :] <= block[:, None], pairs_of[None, :], 0), axis=1)
    rank = jnp.sum(((all_block[:, None] == all_block[None, :]) & (slot[None, :] < slot[:, None])).astype(jnp.int32), axis=1)
    first_pair = jnp.sum(jnp.where(block[None, :] < all_block[:, None], pairs_of[None, :], 0), axis=1)
    position = 2 * first_pair + rank
    positions_most = (slots_all + HALF_BLOCKS + TILES_SLOTS - 1) // TILES_SLOTS * TILES_SLOTS
    positions = jnp.arange(positions_most, dtype=jnp.int32)
    order = slots_all + jnp.sum(jnp.where(position[None, :] == positions[:, None], slot[None, :] - slots_all, 0), axis=1)
    pair_block = jnp.sum((pairs_to[None, :] <= positions[:positions_most // 2, None]).astype(jnp.int32), axis=1)
    pair_block = jnp.minimum(pair_block, HALF_BLOCKS - 1)
    steps = (pairs_to[-1:] + STEP_PAIRS - 1) // STEP_PAIRS

    def spare(values):
        return jnp.pad(values, (0, 8))

    scalars = (order, spare(all_window), spare(all_low), spare(all_high), spare(all_row), spare(all_col % 2), pair_block, steps)
    tiles = tile_parts(scalars, forward_table, spectrum)
    parts = model_parts(scalars, packed, tiles).reshape(band_count, slots_here, VIS_SLOT)
    model = jnp.sum(lax.all_to_all(parts.astype(BF16), "band", 0, 0, tiled=True).astype(F32), axis=0)
    residual = seen.reshape(slots_here, VIS_SLOT) - model
    residual = spread(residual.astype(BF16), band_count).astype(F32).reshape(band_count * tiles_here, 2, VIS_SLOT)
    return gradient_rows(scalars, inverse_table, residual, packed, rows)


def solution(mesh):
    return jax.shard_map(
        on_device,
        mesh=mesh,
        in_specs=(
            P(("parts", "band"), None),
            P(("parts", "band"), None),
            P(("parts", "band")),
            P(("parts", "band"), None),
            P(("parts", "band"), None, None),
            P(("parts", "band"), None, None),
        ),
        out_specs=P(("parts", "band"), None),
        check_vma=False,
    )
```

```python
import functools
import math

import jax
import jax.numpy as jnp
import numpy as np
from jax import lax
from jax.experimental import pallas as pl
from jax.experimental.pallas import tpu as pltpu
from jax.sharding import PartitionSpec as P

RADIX = 128
SIDE = RADIX * RADIX
TILE = 64
HALF_BLOCKS = RADIX // 2
TILE_ROWS = SIDE // TILE
VIS_SLOT = 128
ROW_PITCH = RADIX + 8
ROWS_STEP = 16
STEP_PAIRS = 8
STEP_SLOTS = 2 * STEP_PAIRS
BUFFERS = 4
TILES_PAIRS = 16
TILES_SLOTS = 2 * TILES_PAIRS
RESIDENT_BYTES = 16 << 20
F32 = jnp.float32
BF16 = jnp.bfloat16
NT = (((1,), (1,)), ((), ()))
MIB = 1 << 20


def dot(a, b):
    return jnp.dot(a, b, preferred_element_type=F32)


def dot_nt(a, b):
    return lax.dot_general(a, b, NT, preferred_element_type=F32)


def radix_tables():
    index = np.arange(RADIX)
    angle = (index[:, None] * index[None, :] % RADIX) * (2.0 * math.pi / RADIX)
    turn = (index[:, None] * index[None, :]) * (2.0 * math.pi / SIDE)
    twist = np.concatenate([np.cos(turn), np.sin(turn)]) / RADIX
    return np.cos(angle), np.sin(angle), twist.astype(np.float32)


def whole(shape, space=pltpu.VMEM):
    return pl.BlockSpec(shape, lambda *_: (0,) * len(shape), memory_space=space)


def two_by_two(apart, head_ref, tail_ref, done, twisted):
    def two_rows(i, _):
        first = apart[pl.ds(pl.multiple_of(2 * i * ROW_PITCH, 8), RADIX), :]
        second = apart[pl.ds(pl.multiple_of((2 * i + 1) * ROW_PITCH, 8), RADIX), :]
        mixed = dot(head_ref[...], jnp.concatenate([first, second], axis=1).astype(BF16))
        for side in range(2):
            part = slice(side * RADIX, (side + 1) * RADIX)
            middle = jnp.concatenate(twisted(mixed[:RADIX, part], mixed[RADIX:, part]), axis=1).astype(BF16)
            done[pl.ds(pl.multiple_of((2 * i + side) * ROW_PITCH, 8), RADIX), :] = dot_nt(tail_ref[...], middle)
        return 0

    lax.fori_loop(0, ROWS_STEP // 2, two_rows, 0, unroll=True)


def rows_forward_kernel(sky_ref, head_ref, twist_ref, tail_ref, out_ref, apart, done):
    for a in range(RADIX):
        apart[pl.ds(a, ROWS_STEP, stride=ROW_PITCH), :] = sky_ref[:, a * RADIX:(a + 1) * RADIX].astype(F32)

    def twisted(by_cos, by_sin):
        twist_cos, twist_sin = twist_ref[:RADIX], twist_ref[RADIX:]
        return [by_cos * twist_cos - by_sin * twist_sin, -(by_cos * twist_sin + by_sin * twist_cos)]

    two_by_two(apart, head_ref, tail_ref, done, twisted)
    for j in range(HALF_BLOCKS):
        real = done[pl.ds(j, ROWS_STEP, stride=ROW_PITCH), :]
        imag = done[pl.ds(HALF_BLOCKS + j, ROWS_STEP, stride=ROW_PITCH), :]
        out_ref[j] = jnp.concatenate([real, imag], axis=1).astype(BF16)


def rows_forward(sky):
    rows = sky.shape[0]
    cos, sin, twist = radix_tables()
    head = jnp.asarray(np.concatenate([cos, sin]), BF16)
    tail = jnp.asarray(np.block([[cos[:HALF_BLOCKS], sin[:HALF_BLOCKS]], [-sin[:HALF_BLOCKS], cos[:HALF_BLOCKS]]]), BF16)
    return pl.pallas_call(
        rows_forward_kernel,
        grid=(rows // ROWS_STEP,),
        in_specs=[pl.BlockSpec((ROWS_STEP, SIDE), lambda i: (i, 0)), whole(head.shape), whole(twist.shape), whole(tail.shape)],
        out_specs=pl.BlockSpec((HALF_BLOCKS, ROWS_STEP, 2 * RADIX), lambda i: (0, i, 0)),
        out_shape=jax.ShapeDtypeStruct((HALF_BLOCKS, rows, 2 * RADIX), BF16),
        scratch_shapes=[pltpu.VMEM((ROWS_STEP * ROW_PITCH, RADIX), F32), pltpu.VMEM((ROWS_STEP * ROW_PITCH, RADIX), F32)],
        compiler_params=pltpu.CompilerParams(vmem_limit_bytes=24 * MIB),
        cost_estimate=pl.CostEstimate(flops=rows * RADIX * RADIX * 1024, bytes_accessed=rows * SIDE * 4, transcendentals=0),
        name="rows_forward",
    )(sky, head, jnp.asarray(twist), tail)


def rows_inverse(total, head_ref, twist_ref, tail_ref, out_ref, apart, done, lines, line_sems):
    blocks = out_ref.shape[0] // ROWS_STEP

    def twisted(real, imag):
        twist_cos, twist_sin = twist_ref[:RADIX], twist_ref[RADIX:]
        return [real * twist_cos - imag * twist_sin, real * twist_sin + imag * twist_cos]

    def leave(i):
        buffer = lax.rem(i, 2)
        return pltpu.make_async_copy(lines.at[buffer], out_ref.at[pl.ds(pl.multiple_of(i * ROWS_STEP, ROWS_STEP), ROWS_STEP)], line_sems.at[buffer])

    def one_block(i, _):
        buffer = lax.rem(i, 2)
        rows = pl.ds(pl.multiple_of(i * ROWS_STEP, ROWS_STEP), ROWS_STEP)
        for j in range(HALF_BLOCKS):
            apart[pl.ds(j, ROWS_STEP, stride=ROW_PITCH), :] = total[j, rows, :RADIX]
            apart[pl.ds(HALF_BLOCKS + j, ROWS_STEP, stride=ROW_PITCH), :] = total[j, rows, RADIX:]
        two_by_two(apart, head_ref, tail_ref, done, twisted)

        @pl.when(i >= 2)
        def _():
            leave(i - 2).wait()

        for j in range(RADIX):
            lines[buffer, :, j * RADIX:(j + 1) * RADIX] = done[pl.ds(j, ROWS_STEP, stride=ROW_PITCH), :].astype(BF16)
        leave(i).start()
        return 0

    lax.fori_loop(0, blocks, one_block, 0)
    for back in range(min(2, blocks), 0, -1):
        leave(blocks - back).wait()


def inverse_tables():
    cos, sin, twist = radix_tables()
    used_cos, used_sin = cos[:, :HALF_BLOCKS], sin[:, :HALF_BLOCKS]
    head = np.block([[used_cos, -used_sin], [used_sin, used_cos]])
    tail = np.concatenate([cos, -sin], axis=1)
    return jnp.asarray(head, BF16), jnp.asarray(twist), jnp.asarray(tail, BF16)


def pack_kernel(first_ref, weights_ref, out_ref, lined):
    def one(slot, _):
        lined[pl.ds(first_ref[slot], VIS_SLOT), :] = weights_ref[slot].astype(F32)
        return 0

    lax.fori_loop(0, weights_ref.shape[0], one, 0, unroll=4)
    for tile in range(out_ref.shape[0]):
        out_ref[tile] = lined[tile * VIS_SLOT:(tile + 1) * VIS_SLOT, :].T.astype(BF16)


def pack(first, weights, tiles):
    return pl.pallas_call(
        pack_kernel,
        in_specs=[pl.BlockSpec(memory_space=pltpu.SMEM), pl.BlockSpec(memory_space=pltpu.VMEM)],
        out_specs=pl.BlockSpec(memory_space=pltpu.VMEM),
        out_shape=jax.ShapeDtypeStruct((tiles, 2 * TILE, VIS_SLOT), BF16),
        scratch_shapes=[pltpu.VMEM(((tiles + 1) * VIS_SLOT, 2 * TILE), F32)],
        compiler_params=pltpu.CompilerParams(vmem_limit_bytes=16 * MIB),
        cost_estimate=pl.CostEstimate(flops=0, bytes_accessed=4 * MIB, transcendentals=0),
        name="pack",
    )(first, weights)


def line_up_kernel(first_ref, observed_ref, seen_ref):
    column = lax.broadcasted_iota(jnp.int32, (8, VIS_SLOT), 1)

    def one(slot, _):
        tile, shift = first_ref[slot] // VIS_SLOT, first_ref[slot] % VIS_SLOT
        turned = pltpu.roll(observed_ref[slot], shift, 1)
        seen_ref[tile] = jnp.where(column >= shift, turned, seen_ref[tile])
        seen_ref[tile + 1] = turned
        return 0

    lax.fori_loop(0, observed_ref.shape[0], one, 0)


def line_up(first, observed, tiles):
    padded = jnp.pad(observed.astype(F32), ((0, 0), (0, 6), (0, 0)))
    seen = pl.pallas_call(
        line_up_kernel,
        in_specs=[pl.BlockSpec(memory_space=pltpu.SMEM), pl.BlockSpec(memory_space=pltpu.VMEM)],
        out_specs=pl.BlockSpec(memory_space=pltpu.VMEM),
        out_shape=jax.ShapeDtypeStruct((tiles + 1, 8, VIS_SLOT), F32),
        name="line_up",
    )(first, padded)
    return seen[:tiles, :2]


def tiles_kernel(order_ref, row_ref, block_ref, steps_ref, table_ref, spectrum_ref, out_ref, ready, sems):
    steps = (steps_ref[0] * STEP_PAIRS + TILES_PAIRS - 1) // TILES_PAIRS

    def leave(step, buffer):
        return pltpu.make_async_copy(ready.at[buffer], out_ref.at[pl.ds(step * TILES_SLOTS, TILES_SLOTS)], sems.at[buffer])

    def step_body(step, _):
        buffer = lax.rem(step, BUFFERS)

        @pl.when(step >= BUFFERS)
        def _():
            leave(step - BUFFERS, buffer).wait()

        for pair in range(TILES_PAIRS):
            slots = [order_ref[step * TILES_SLOTS + 2 * pair + i] for i in range(2)]
            columns = spectrum_ref[block_ref[step * TILES_PAIRS + pair]]
            tables = jnp.concatenate([table_ref[row_ref[slot]] for slot in slots], axis=0)
            turned = dot(tables, columns)
            for i in range(2):
                base = 2 * TILE * i
                by_cos, by_sin = turned[base:base + TILE], turned[base + TILE:base + 2 * TILE]
                ready[buffer, 2 * pair + i, :TILE] = (by_cos[:, :RADIX] + by_sin[:, RADIX:]).astype(BF16)
                ready[buffer, 2 * pair + i, TILE:] = (by_cos[:, RADIX:] - by_sin[:, :RADIX]).astype(BF16)
        leave(step, buffer).start()
        return 0

    lax.fori_loop(0, steps, step_body, 0)
    for back in range(BUFFERS, 0, -1):
        leave(steps - back, lax.rem(steps - back, BUFFERS)).wait()


def tile_parts(scalars, table, spectrum):
    order, window, low, high, row, half, block, steps = scalars
    return pl.pallas_call(
        tiles_kernel,
        in_specs=[pl.BlockSpec(memory_space=pltpu.SMEM)] * 4 + [pl.BlockSpec(memory_space=pltpu.VMEM)] * 2,
        out_specs=pl.BlockSpec(memory_space=pl.ANY),
        out_shape=jax.ShapeDtypeStruct((order.shape[0], 2 * TILE, RADIX), BF16),
        scratch_shapes=[pltpu.VMEM((BUFFERS, TILES_SLOTS, 2 * TILE, RADIX), BF16), pltpu.SemaphoreType.DMA((BUFFERS,))],
        compiler_params=pltpu.CompilerParams(vmem_limit_bytes=30 * MIB),
        cost_estimate=pl.CostEstimate(flops=order.shape[0] * RADIX ** 3 * 8, bytes_accessed=64 * MIB, transcendentals=0),
        name="tiles",
    )(order, row, block, steps, table, spectrum)


def copies(scalars, packed_ref, v_ref, u_ref, sems, step, buffer):
    order_ref, window_ref, half_ref = scalars
    started = []
    for i in range(STEP_SLOTS):
        slot = order_ref[step * STEP_SLOTS + i]
        window = window_ref[slot]
        half = half_ref[slot]
        from_row = pl.multiple_of(half * TILE, TILE)
        started.append(pltpu.make_async_copy(packed_ref.at[pl.ds(window, 2), :TILE], v_ref.at[buffer, i], sems.at[buffer, i, 0]))
        started.append(pltpu.make_async_copy(packed_ref.at[pl.ds(window, 2), TILE:], u_ref.at[buffer, i, half, :, pl.ds(from_row, TILE)], sems.at[buffer, i, 1]))
    return started


def over_steps(steps, fetch, work):
    ahead = BUFFERS - 1
    for step in range(ahead):
        for copy in fetch(step, step):
            copy.start()

    def step_body(step, _):
        buffer = lax.rem(step, BUFFERS)

        @pl.when(step + ahead < steps)
        def _():
            for copy in fetch(step + ahead, lax.rem(step + ahead, BUFFERS)):
                copy.start()

        for copy in fetch(step, buffer):
            copy.wait()
        work(step, buffer)
        return 0

    lax.fori_loop(0, steps, step_body, 0)


def clear_sides(u_ref):
    for buffer in range(BUFFERS):
        for i in range(STEP_SLOTS):
            u_ref[buffer, i] = jnp.zeros(u_ref.shape[2:], BF16)


def side_by_side(pair):
    return jnp.concatenate([pair[0], pair[1]], axis=1)


def model_kernel(resident, order_ref, window_ref, low_ref, high_ref, half_ref, steps_ref, packed_ref, tiles_ref, out_ref, t_ref, t_sems, *buffers):
    column = lax.broadcasted_iota(jnp.int32, (1, 2 * VIS_SLOT), 1)
    if not resident:
        v_ref, u_ref, sems = buffers
        clear_sides(u_ref)

    def fetch(step, buffer):
        started = [pltpu.make_async_copy(tiles_ref.at[pl.ds(step * STEP_SLOTS, STEP_SLOTS)], t_ref.at[buffer], t_sems.at[buffer])]
        if not resident:
            started += copies((order_ref, window_ref, half_ref), packed_ref, v_ref, u_ref, sems, step, buffer)
        return started

    def weights(i, slot, buffer):
        if not resident:
            return side_by_side(v_ref[buffer, i]), side_by_side(u_ref[buffer, i, half_ref[slot]])
        window = window_ref[slot]
        along_v = side_by_side([packed_ref[window, :TILE], packed_ref[window + 1, :TILE]])
        along_u = side_by_side([packed_ref[window, TILE:], packed_ref[window + 1, TILE:]])
        none = jnp.zeros_like(along_u)
        upper = half_ref[slot] == 1
        return along_v, jnp.concatenate([jnp.where(upper, none, along_u), jnp.where(upper, along_u, none)], axis=0)

    def work(step, buffer):
        found = []
        for i in range(STEP_SLOTS):
            slot = order_ref[step * STEP_SLOTS + i]
            weights_v, weights_u = weights(i, slot, buffer)
            inner = dot(t_ref[buffer, i], weights_u)
            weights_v = weights_v.astype(F32)
            real = jnp.sum(inner[:TILE] * weights_v, axis=0, keepdims=True)
            imag = jnp.sum(inner[TILE:] * weights_v, axis=0, keepdims=True)
            mine = (column >= low_ref[slot]) & (column < high_ref[slot])
            found.append((window_ref[slot], mine, jnp.concatenate([real, imag], axis=0)))
        for window, mine, both in found:
            out_ref[window] = jnp.where(mine[:, :VIS_SLOT], both[:, :VIS_SLOT], out_ref[window])
            out_ref[window + 1] = jnp.where(mine[:, VIS_SLOT:], both[:, VIS_SLOT:], out_ref[window + 1])

    over_steps(steps_ref[0], fetch, work)


def slot_buffers():
    return [
        pltpu.VMEM((BUFFERS, STEP_SLOTS, 2, TILE, VIS_SLOT), BF16),
        pltpu.VMEM((BUFFERS, STEP_SLOTS, 2, 2, 2 * TILE, VIS_SLOT), BF16),
    ]


def model_parts(scalars, packed, tiles):
    order, window, low, high, row, half, block, steps = scalars
    resident = packed.size * 2 <= RESIDENT_BYTES
    buffers = [] if resident else slot_buffers() + [pltpu.SemaphoreType.DMA((BUFFERS, STEP_SLOTS, 2))]
    return pl.pallas_call(
        functools.partial(model_kernel, resident),
        in_specs=[pl.BlockSpec(memory_space=pltpu.SMEM)] * 6 + [pl.BlockSpec(memory_space=pltpu.VMEM if resident else pl.ANY), pl.BlockSpec(memory_space=pl.ANY)],
        out_specs=pl.BlockSpec(memory_space=pltpu.VMEM),
        out_shape=jax.ShapeDtypeStruct((packed.shape[0], 2, VIS_SLOT), F32),
        scratch_shapes=[pltpu.VMEM((BUFFERS, STEP_SLOTS, 2 * TILE, RADIX), BF16), pltpu.SemaphoreType.DMA((BUFFERS,))] + buffers,
        compiler_params=pltpu.CompilerParams(vmem_limit_bytes=22 * MIB),
        cost_estimate=pl.CostEstimate(flops=order.shape[0] * RADIX ** 3 * 4, bytes_accessed=96 * MIB, transcendentals=0),
        name="model",
    )(order, window, low, high, half, steps, packed, tiles)


def gradient_kernel(order_ref, window_ref, low_ref, high_ref, row_ref, half_ref, block_ref, steps_ref, table_ref, residual_ref, head_ref, twist_ref, tail_ref, packed_ref, out_ref, total, blocks_ref, sems, *lines):
    column = lax.broadcasted_iota(jnp.int32, (1, 2 * VIS_SLOT), 1)
    sign = jnp.where(lax.broadcasted_iota(jnp.int32, (1, 2 * TILE), 1) < TILE, 1.0, -1.0)

    def clear(j, _):
        total[j] = jnp.zeros(total.shape[1:], F32)
        return 0

    lax.fori_loop(0, HALF_BLOCKS, clear, 0)

    def fetch(step, buffer):
        started = []
        for i in range(STEP_SLOTS):
            window = window_ref[order_ref[step * STEP_SLOTS + i]]
            started.append(pltpu.make_async_copy(packed_ref.at[pl.ds(window, 2)], blocks_ref.at[buffer, i], sems.at[buffer, i]))
        return started

    def work(step, buffer):
        found = []
        for pair in range(STEP_PAIRS):
            slots = [order_ref[step * STEP_SLOTS + 2 * pair + i] for i in range(2)]
            tiles = []
            for i, slot in enumerate(slots):
                at = 2 * pair + i
                window = window_ref[slot]
                mine = (column >= low_ref[slot]) & (column < high_ref[slot])
                residual = side_by_side([residual_ref[window], residual_ref[window + 1]])
                residual = jnp.where(mine, residual, 0.0)
                weights_v = side_by_side([blocks_ref[buffer, at, 0, :TILE], blocks_ref[buffer, at, 1, :TILE]]).astype(F32)
                weights_u = side_by_side([blocks_ref[buffer, at, 0, TILE:], blocks_ref[buffer, at, 1, TILE:]])
                weighted = jnp.concatenate([weights_v * residual[0:1], weights_v * residual[1:2]], axis=0).astype(BF16)
                tile = dot_nt(weights_u, weighted)
                real, imag = (tile * sign).astype(BF16), pltpu.roll(tile, TILE, 1).astype(BF16)
                none = jnp.zeros_like(real)
                upper = half_ref[slot] == 1
                tiles.append(jnp.concatenate([
                    jnp.where(upper, none, real), jnp.where(upper, real, none),
                    jnp.where(upper, none, imag), jnp.where(upper, imag, none),
                ], axis=0))
            found.append((slots, jnp.concatenate(tiles, axis=1)))
        for pair, (slots, both) in enumerate(found):
            tables = jnp.concatenate([table_ref[row_ref[slot]] for slot in slots], axis=1)
            block = block_ref[step * STEP_PAIRS + pair]
            total[block] = total[block] + dot_nt(tables, both)

    over_steps(steps_ref[0], fetch, work)
    rows_inverse(total, head_ref, twist_ref, tail_ref, out_ref, *lines)


def gradient_rows(scalars, table, residual, packed, rows):
    return pl.pallas_call(
        gradient_kernel,
        in_specs=[pl.BlockSpec(memory_space=pltpu.SMEM)] * 8 + [pl.BlockSpec(memory_space=pltpu.VMEM)] * 5 + [pl.BlockSpec(memory_space=pl.ANY)],
        out_specs=pl.BlockSpec(memory_space=pl.ANY),
        out_shape=jax.ShapeDtypeStruct((rows, SIDE), BF16),
        scratch_shapes=[pltpu.VMEM((HALF_BLOCKS, rows, 2 * RADIX), F32)] + [
            pltpu.VMEM((BUFFERS, STEP_SLOTS, 2, 2 * TILE, VIS_SLOT), BF16),
            pltpu.SemaphoreType.DMA((BUFFERS, STEP_SLOTS)),
            pltpu.VMEM((ROWS_STEP * ROW_PITCH, RADIX), F32),
            pltpu.VMEM((ROWS_STEP * ROW_PITCH, RADIX), F32),
            pltpu.VMEM((2, ROWS_STEP, SIDE), BF16),
            pltpu.SemaphoreType.DMA((2,)),
        ],
        compiler_params=pltpu.CompilerParams(vmem_limit_bytes=36 * MIB),
        cost_estimate=pl.CostEstimate(flops=scalars[0].shape[0] * RADIX ** 3 * 8, bytes_accessed=96 * MIB, transcendentals=0),
        name="gradient",
    )(*scalars, table, residual, *inverse_tables(), packed)


def column_tables(first_row, rows):
    y = first_row + jnp.arange(rows, dtype=jnp.int32)
    r = jnp.arange(TILE_ROWS, dtype=jnp.int32)
    a = jnp.arange(TILE, dtype=jnp.int32)
    coarse = (r[:, None] * y[None, :] % TILE_ROWS).astype(F32) * (2.0 * math.pi / TILE_ROWS)
    fine = (a[:, None] * y[None, :] % SIDE).astype(F32) * (2.0 * math.pi / SIDE)
    coarse_cos, coarse_sin = jnp.cos(coarse), jnp.sin(coarse)
    fine_cos, fine_sin = jnp.cos(fine) / RADIX, jnp.sin(fine) / RADIX
    with_cos = jnp.concatenate([fine_cos, fine_sin])
    with_sin = jnp.concatenate([fine_sin, -fine_cos])
    forward = coarse_cos[:, None, :] * with_cos[None] - coarse_sin[:, None, :] * with_sin[None]
    inverse = coarse_cos[:, :, None] * with_cos.T[None] - coarse_sin[:, :, None] * with_sin.T[None]
    return lax.optimization_barrier((forward.astype(BF16), inverse.astype(BF16)))


def firsts(counts):
    slot = jnp.arange(counts.shape[1], dtype=jnp.int32)
    ahead = slot[None, None, :] < slot[None, :, None]
    return jnp.sum(jnp.where(ahead, counts[:, None, :], 0), axis=2)


def spread(values, band_count):
    return lax.all_to_all(jnp.broadcast_to(values[None], (band_count,) + values.shape), "band", 0, 0, tiled=True)


def on_device(sky_image, tile_band, tile_place, counts, kernel, observed):
    band_count = lax.axis_size("band")
    rows = sky_image.shape[0]
    slots_here = tile_place.shape[0]
    slots_all = band_count * slots_here
    tiles_across = sky_image.shape[1] // 2 // band_count // TILE
    tiles_here = slots_here // 2

    tile_row = tile_place // tiles_across
    tile_col = tile_band[:, 0] * tiles_across + tile_place % tiles_across
    first = firsts(counts)[0]
    packed = lax.all_gather(pack(first, kernel, tiles_here), "band", tiled=True)
    seen = line_up(first, observed, tiles_here)

    every = spread(jnp.stack([tile_row, tile_col, counts[0]]), band_count)
    all_row, all_col = (every[:, i].reshape(slots_all) for i in range(2))
    all_block = all_col // 2
    all_first = firsts(every[:, 2])
    all_window = jnp.minimum(all_first // VIS_SLOT, tiles_here - 2)
    all_low = all_first - all_window * VIS_SLOT
    all_high = (all_low + every[:, 2]).reshape(slots_all)
    all_low = all_low.reshape(slots_all)
    all_window = (all_window + tiles_here * jnp.arange(band_count, dtype=jnp.int32)[:, None]).reshape(slots_all)

    spectrum = rows_forward(sky_image)
    forward_table, inverse_table = column_tables(lax.axis_index("band").astype(jnp.int32) * rows, rows)

    slot = jnp.arange(slots_all, dtype=jnp.int32)
    block = jnp.arange(HALF_BLOCKS, dtype=jnp.int32)
    in_block = jnp.sum((all_block[:, None] == block[None, :]).astype(jnp.int32), axis=0)
    pairs_of = (in_block + 1) // 2
    pairs_to = jnp.sum(jnp.where(block[None, :] <= block[:, None], pairs_of[None, :], 0), axis=1)
    rank = jnp.sum(((all_block[:, None] == all_block[None, :]) & (slot[None, :] < slot[:, None])).astype(jnp.int32), axis=1)
    first_pair = jnp.sum(jnp.where(block[None, :] < all_block[:, None], pairs_of[None, :], 0), axis=1)
    position = 2 * first_pair + rank
    positions_most = (slots_all + HALF_BLOCKS + TILES_SLOTS - 1) // TILES_SLOTS * TILES_SLOTS
    positions = jnp.arange(positions_most, dtype=jnp.int32)
    order = slots_all + jnp.sum(jnp.where(position[None, :] == positions[:, None], slot[None, :] - slots_all, 0), axis=1)
    pair_block = jnp.sum((pairs_to[None, :] <= positions[:positions_most // 2, None]).astype(jnp.int32), axis=1)
    pair_block = jnp.minimum(pair_block, HALF_BLOCKS - 1)
    steps = (pairs_to[-1:] + STEP_PAIRS - 1) // STEP_PAIRS

    def spare(values):
        return jnp.pad(values, (0, 8))

    scalars = (order, spare(all_window), spare(all_low), spare(all_high), spare(all_row), spare(all_col % 2), pair_block, steps)
    tiles = tile_parts(scalars, forward_table, spectrum)
    parts = model_parts(scalars, packed, tiles).reshape(band_count, slots_here, VIS_SLOT)
    model = jnp.sum(lax.all_to_all(parts.astype(BF16), "band", 0, 0, tiled=True).astype(F32), axis=0)
    residual = seen.reshape(slots_here, VIS_SLOT) - model
    residual = spread(residual.astype(BF16), band_count).astype(F32).reshape(band_count * tiles_here, 2, VIS_SLOT)
    return gradient_rows(scalars, inverse_table, residual, packed, rows)


def solution(mesh):
    return jax.shard_map(
        on_device,
        mesh=mesh,
        in_specs=(
            P(("parts", "band"), None),
            P(("parts", "band"), None),
            P(("parts", "band")),
            P(("parts", "band"), None),
            P(("parts", "band"), None, None),
            P(("parts", "band"), None, None),
        ),
        out_specs=P(("parts", "band"), None),
        check_vma=False,
    )
```

```python
import functools
import math

import jax
import jax.numpy as jnp
import numpy as np
from jax import lax
from jax.experimental import pallas as pl
from jax.experimental.pallas import tpu as pltpu
from jax.sharding import PartitionSpec as P

RADIX = 128
SIDE = RADIX * RADIX
TILE = 64
HALF_BLOCKS = RADIX // 2
TILE_ROWS = SIDE // TILE
VIS_SLOT = 128
ROW_PITCH = RADIX + 8
ROWS_STEP = 16
STEP_PAIRS = 8
STEP_SLOTS = 2 * STEP_PAIRS
BUFFERS = 4
TILES_PAIRS = 16
TILES_SLOTS = 2 * TILES_PAIRS
RESIDENT_BYTES = 16 << 20
F32 = jnp.float32
BF16 = jnp.bfloat16
NT = (((1,), (1,)), ((), ()))
MIB = 1 << 20


def dot(a, b):
    return jnp.dot(a, b, preferred_element_type=F32)


def dot_nt(a, b):
    return lax.dot_general(a, b, NT, preferred_element_type=F32)


def radix_tables():
    index = np.arange(RADIX)
    angle = (index[:, None] * index[None, :] % RADIX) * (2.0 * math.pi / RADIX)
    turn = (index[:, None] * index[None, :]) * (2.0 * math.pi / SIDE)
    twist = np.concatenate([np.cos(turn), np.sin(turn)]) / RADIX
    return np.cos(angle), np.sin(angle), twist.astype(np.float32)


def whole(shape, space=pltpu.VMEM):
    return pl.BlockSpec(shape, lambda *_: (0,) * len(shape), memory_space=space)


def two_by_two(apart, head_ref, tail_ref, done, twisted):
    def two_rows(i, _):
        first = apart[pl.ds(pl.multiple_of(2 * i * ROW_PITCH, 8), RADIX), :]
        second = apart[pl.ds(pl.multiple_of((2 * i + 1) * ROW_PITCH, 8), RADIX), :]
        mixed = dot(head_ref[...], jnp.concatenate([first, second], axis=1).astype(BF16))
        for side in range(2):
            part = slice(side * RADIX, (side + 1) * RADIX)
            middle = jnp.concatenate(twisted(mixed[:RADIX, part], mixed[RADIX:, part]), axis=1).astype(BF16)
            done[pl.ds(pl.multiple_of((2 * i + side) * ROW_PITCH, 8), RADIX), :] = dot_nt(tail_ref[...], middle)
        return 0

    lax.fori_loop(0, ROWS_STEP // 2, two_rows, 0, unroll=True)


def rows_forward_kernel(sky_ref, head_ref, twist_ref, tail_ref, out_ref, apart, done):
    for a in range(RADIX):
        apart[pl.ds(a, ROWS_STEP, stride=ROW_PITCH), :] = sky_ref[:, a * RADIX:(a + 1) * RADIX].astype(F32)

    def twisted(by_cos, by_sin):
        twist_cos, twist_sin = twist_ref[:RADIX], twist_ref[RADIX:]
        return [by_cos * twist_cos - by_sin * twist_sin, -(by_cos * twist_sin + by_sin * twist_cos)]

    two_by_two(apart, head_ref, tail_ref, done, twisted)
    for j in range(HALF_BLOCKS):
        real = done[pl.ds(j, ROWS_STEP, stride=ROW_PITCH), :]
        imag = done[pl.ds(HALF_BLOCKS + j, ROWS_STEP, stride=ROW_PITCH), :]
        out_ref[j] = jnp.concatenate([real, imag], axis=1).astype(BF16)


def rows_forward(sky):
    rows = sky.shape[0]
    cos, sin, twist = radix_tables()
    head = jnp.asarray(np.concatenate([cos, sin]), BF16)
    tail = jnp.asarray(np.block([[cos[:HALF_BLOCKS], sin[:HALF_BLOCKS]], [-sin[:HALF_BLOCKS], cos[:HALF_BLOCKS]]]), BF16)
    return pl.pallas_call(
        rows_forward_kernel,
        grid=(rows // ROWS_STEP,),
        in_specs=[pl.BlockSpec((ROWS_STEP, SIDE), lambda i: (i, 0)), whole(head.shape), whole(twist.shape), whole(tail.shape)],
        out_specs=pl.BlockSpec((HALF_BLOCKS, ROWS_STEP, 2 * RADIX), lambda i: (0, i, 0)),
        out_shape=jax.ShapeDtypeStruct((HALF_BLOCKS, rows, 2 * RADIX), BF16),
        scratch_shapes=[pltpu.VMEM((ROWS_STEP * ROW_PITCH, RADIX), F32), pltpu.VMEM((ROWS_STEP * ROW_PITCH, RADIX), F32)],
        compiler_params=pltpu.CompilerParams(vmem_limit_bytes=24 * MIB),
        cost_estimate=pl.CostEstimate(flops=rows * RADIX * RADIX * 1024, bytes_accessed=rows * SIDE * 4, transcendentals=0),
        name="rows_forward",
    )(sky, head, jnp.asarray(twist), tail)


def rows_inverse(total, head_ref, twist_ref, tail_ref, out_ref, apart, done, lines, line_sems):
    blocks = out_ref.shape[0] // ROWS_STEP

    def twisted(real, imag):
        twist_cos, twist_sin = twist_ref[:RADIX], twist_ref[RADIX:]
        return [real * twist_cos - imag * twist_sin, real * twist_sin + imag * twist_cos]

    def leave(i):
        buffer = lax.rem(i, 2)
        return pltpu.make_async_copy(lines.at[buffer], out_ref.at[pl.ds(pl.multiple_of(i * ROWS_STEP, ROWS_STEP), ROWS_STEP)], line_sems.at[buffer])

    def one_block(i, _):
        buffer = lax.rem(i, 2)
        rows = pl.ds(pl.multiple_of(i * ROWS_STEP, ROWS_STEP), ROWS_STEP)
        for j in range(HALF_BLOCKS):
            apart[pl.ds(j, ROWS_STEP, stride=ROW_PITCH), :] = total[j, rows, :RADIX]
            apart[pl.ds(HALF_BLOCKS + j, ROWS_STEP, stride=ROW_PITCH), :] = total[j, rows, RADIX:]
        two_by_two(apart, head_ref, tail_ref, done, twisted)

        @pl.when(i >= 2)
        def _():
            leave(i - 2).wait()

        for j in range(RADIX):
            lines[buffer, :, j * RADIX:(j + 1) * RADIX] = done[pl.ds(j, ROWS_STEP, stride=ROW_PITCH), :].astype(BF16)
        leave(i).start()
        return 0

    lax.fori_loop(0, blocks, one_block, 0)
    for back in range(min(2, blocks), 0, -1):
        leave(blocks - back).wait()


def inverse_tables():
    cos, sin, twist = radix_tables()
    used_cos, used_sin = cos[:, :HALF_BLOCKS], sin[:, :HALF_BLOCKS]
    head = np.block([[used_cos, -used_sin], [used_sin, used_cos]])
    tail = np.concatenate([cos, -sin], axis=1)
    return jnp.asarray(head, BF16), jnp.asarray(twist), jnp.asarray(tail, BF16)


def pack_kernel(first_ref, weights_ref, out_ref, lined):
    def one(slot, _):
        lined[pl.ds(first_ref[slot], VIS_SLOT), :] = weights_ref[slot].astype(F32)
        return 0

    lax.fori_loop(0, weights_ref.shape[0], one, 0, unroll=4)
    for tile in range(out_ref.shape[0]):
        out_ref[tile] = lined[tile * VIS_SLOT:(tile + 1) * VIS_SLOT, :].T.astype(BF16)


def pack(first, weights, tiles):
    return pl.pallas_call(
        pack_kernel,
        in_specs=[pl.BlockSpec(memory_space=pltpu.SMEM), pl.BlockSpec(memory_space=pltpu.VMEM)],
        out_specs=pl.BlockSpec(memory_space=pltpu.VMEM),
        out_shape=jax.ShapeDtypeStruct((tiles, 2 * TILE, VIS_SLOT), BF16),
        scratch_shapes=[pltpu.VMEM(((tiles + 1) * VIS_SLOT, 2 * TILE), F32)],
        compiler_params=pltpu.CompilerParams(vmem_limit_bytes=16 * MIB),
        cost_estimate=pl.CostEstimate(flops=0, bytes_accessed=4 * MIB, transcendentals=0),
        name="pack",
    )(first, weights)


def line_up_kernel(first_ref, observed_ref, seen_ref):
    column = lax.broadcasted_iota(jnp.int32, (8, VIS_SLOT), 1)

    def one(slot, _):
        tile, shift = first_ref[slot] // VIS_SLOT, first_ref[slot] % VIS_SLOT
        turned = pltpu.roll(observed_ref[slot], shift, 1)
        seen_ref[tile] = jnp.where(column >= shift, turned, seen_ref[tile])
        seen_ref[tile + 1] = turned
        return 0

    lax.fori_loop(0, observed_ref.shape[0], one, 0)


def line_up(first, observed, tiles):
    padded = jnp.pad(observed.astype(F32), ((0, 0), (0, 6), (0, 0)))
    seen = pl.pallas_call(
        line_up_kernel,
        in_specs=[pl.BlockSpec(memory_space=pltpu.SMEM), pl.BlockSpec(memory_space=pltpu.VMEM)],
        out_specs=pl.BlockSpec(memory_space=pltpu.VMEM),
        out_shape=jax.ShapeDtypeStruct((tiles + 1, 8, VIS_SLOT), F32),
        name="line_up",
    )(first, padded)
    return seen[:tiles, :2]


def tiles_kernel(order_ref, row_ref, block_ref, steps_ref, table_ref, spectrum_ref, out_ref, ready, sems):
    steps = (steps_ref[0] * STEP_PAIRS + TILES_PAIRS - 1) // TILES_PAIRS

    def leave(step, buffer):
        return pltpu.make_async_copy(ready.at[buffer], out_ref.at[pl.ds(step * TILES_SLOTS, TILES_SLOTS)], sems.at[buffer])

    def step_body(step, _):
        buffer = lax.rem(step, BUFFERS)

        @pl.when(step >= BUFFERS)
        def _():
            leave(step - BUFFERS, buffer).wait()

        for pair in range(TILES_PAIRS):
            slots = [order_ref[step * TILES_SLOTS + 2 * pair + i] for i in range(2)]
            columns = spectrum_ref[block_ref[step * TILES_PAIRS + pair]]
            tables = jnp.concatenate([table_ref[row_ref[slot]] for slot in slots], axis=0)
            turned = dot(tables, columns)
            for i in range(2):
                base = 2 * TILE * i
                by_cos, by_sin = turned[base:base + TILE], turned[base + TILE:base + 2 * TILE]
                ready[buffer, 2 * pair + i, :TILE] = (by_cos[:, :RADIX] + by_sin[:, RADIX:]).astype(BF16)
                ready[buffer, 2 * pair + i, TILE:] = (by_cos[:, RADIX:] - by_sin[:, :RADIX]).astype(BF16)
        leave(step, buffer).start()
        return 0

    lax.fori_loop(0, steps, step_body, 0)
    for back in range(BUFFERS, 0, -1):
        leave(steps - back, lax.rem(steps - back, BUFFERS)).wait()


def tile_parts(scalars, table, spectrum):
    order, window, low, high, row, half, block, steps = scalars
    return pl.pallas_call(
        tiles_kernel,
        in_specs=[pl.BlockSpec(memory_space=pltpu.SMEM)] * 4 + [pl.BlockSpec(memory_space=pltpu.VMEM)] * 2,
        out_specs=pl.BlockSpec(memory_space=pl.ANY),
        out_shape=jax.ShapeDtypeStruct((order.shape[0], 2 * TILE, RADIX), BF16),
        scratch_shapes=[pltpu.VMEM((BUFFERS, TILES_SLOTS, 2 * TILE, RADIX), BF16), pltpu.SemaphoreType.DMA((BUFFERS,))],
        compiler_params=pltpu.CompilerParams(vmem_limit_bytes=30 * MIB),
        cost_estimate=pl.CostEstimate(flops=order.shape[0] * RADIX ** 3 * 8, bytes_accessed=64 * MIB, transcendentals=0),
        name="tiles",
    )(order, row, block, steps, table, spectrum)


def copies(scalars, packed_ref, v_ref, u_ref, sems, step, buffer):
    order_ref, window_ref, half_ref = scalars
    started = []
    for i in range(STEP_SLOTS):
        slot = order_ref[step * STEP_SLOTS + i]
        window = window_ref[slot]
        half = half_ref[slot]
        from_row = pl.multiple_of(half * TILE, TILE)
        started.append(pltpu.make_async_copy(packed_ref.at[pl.ds(window, 2), :TILE], v_ref.at[buffer, i], sems.at[buffer, i, 0]))
        started.append(pltpu.make_async_copy(packed_ref.at[pl.ds(window, 2), TILE:], u_ref.at[buffer, i, half, :, pl.ds(from_row, TILE)], sems.at[buffer, i, 1]))
    return started


def over_steps(steps, fetch, work):
    ahead = BUFFERS - 1
    for step in range(ahead):
        for copy in fetch(step, step):
            copy.start()

    def step_body(step, _):
        buffer = lax.rem(step, BUFFERS)

        @pl.when(step + ahead < steps)
        def _():
            for copy in fetch(step + ahead, lax.rem(step + ahead, BUFFERS)):
                copy.start()

        for copy in fetch(step, buffer):
            copy.wait()
        work(step, buffer)
        return 0

    lax.fori_loop(0, steps, step_body, 0)


def clear_sides(u_ref):
    for buffer in range(BUFFERS):
        for i in range(STEP_SLOTS):
            u_ref[buffer, i] = jnp.zeros(u_ref.shape[2:], BF16)


def side_by_side(pair):
    return jnp.concatenate([pair[0], pair[1]], axis=1)


def model_kernel(resident, order_ref, window_ref, low_ref, high_ref, half_ref, steps_ref, packed_ref, tiles_ref, out_ref, t_ref, t_sems, *buffers):
    column = lax.broadcasted_iota(jnp.int32, (1, 2 * VIS_SLOT), 1)
    if not resident:
        v_ref, u_ref, sems = buffers
        clear_sides(u_ref)

    def fetch(step, buffer):
        started = [pltpu.make_async_copy(tiles_ref.at[pl.ds(step * STEP_SLOTS, STEP_SLOTS)], t_ref.at[buffer], t_sems.at[buffer])]
        if not resident:
            started += copies((order_ref, window_ref, half_ref), packed_ref, v_ref, u_ref, sems, step, buffer)
        return started

    def weights(i, slot, buffer):
        if not resident:
            return side_by_side(v_ref[buffer, i]), side_by_side(u_ref[buffer, i, half_ref[slot]])
        window = window_ref[slot]
        along_v = side_by_side([packed_ref[window, :TILE], packed_ref[window + 1, :TILE]])
        along_u = side_by_side([packed_ref[window, TILE:], packed_ref[window + 1, TILE:]])
        none = jnp.zeros_like(along_u)
        upper = half_ref[slot] == 1
        return along_v, jnp.concatenate([jnp.where(upper, none, along_u), jnp.where(upper, along_u, none)], axis=0)

    def work(step, buffer):
        found = []
        for i in range(STEP_SLOTS):
            slot = order_ref[step * STEP_SLOTS + i]
            weights_v, weights_u = weights(i, slot, buffer)
            inner = dot(t_ref[buffer, i], weights_u)
            weights_v = weights_v.astype(F32)
            real = jnp.sum(inner[:TILE] * weights_v, axis=0, keepdims=True)
            imag = jnp.sum(inner[TILE:] * weights_v, axis=0, keepdims=True)
            mine = (column >= low_ref[slot]) & (column < high_ref[slot])
            found.append((window_ref[slot], mine, jnp.concatenate([real, imag], axis=0)))
        for window, mine, both in found:
            out_ref[window] = jnp.where(mine[:, :VIS_SLOT], both[:, :VIS_SLOT], out_ref[window])
            out_ref[window + 1] = jnp.where(mine[:, VIS_SLOT:], both[:, VIS_SLOT:], out_ref[window + 1])

    over_steps(steps_ref[0], fetch, work)


def slot_buffers():
    return [
        pltpu.VMEM((BUFFERS, STEP_SLOTS, 2, TILE, VIS_SLOT), BF16),
        pltpu.VMEM((BUFFERS, STEP_SLOTS, 2, 2, 2 * TILE, VIS_SLOT), BF16),
    ]


def model_parts(scalars, packed, tiles):
    order, window, low, high, row, half, block, steps = scalars
    resident = packed.size * 2 <= RESIDENT_BYTES
    buffers = [] if resident else slot_buffers() + [pltpu.SemaphoreType.DMA((BUFFERS, STEP_SLOTS, 2))]
    return pl.pallas_call(
        functools.partial(model_kernel, resident),
        in_specs=[pl.BlockSpec(memory_space=pltpu.SMEM)] * 6 + [pl.BlockSpec(memory_space=pltpu.VMEM if resident else pl.ANY), pl.BlockSpec(memory_space=pl.ANY)],
        out_specs=pl.BlockSpec(memory_space=pltpu.VMEM),
        out_shape=jax.ShapeDtypeStruct((packed.shape[0], 2, VIS_SLOT), F32),
        scratch_shapes=[pltpu.VMEM((BUFFERS, STEP_SLOTS, 2 * TILE, RADIX), BF16), pltpu.SemaphoreType.DMA((BUFFERS,))] + buffers,
        compiler_params=pltpu.CompilerParams(vmem_limit_bytes=22 * MIB),
        cost_estimate=pl.CostEstimate(flops=order.shape[0] * RADIX ** 3 * 4, bytes_accessed=96 * MIB, transcendentals=0),
        name="model",
    )(order, window, low, high, half, steps, packed, tiles)


def gradient_kernel(order_ref, window_ref, low_ref, high_ref, row_ref, half_ref, block_ref, steps_ref, table_ref, residual_ref, head_ref, twist_ref, tail_ref, packed_ref, out_ref, total, v_ref, u_ref, sems, *lines):
    column = lax.broadcasted_iota(jnp.int32, (1, 2 * VIS_SLOT), 1)
    clear_sides(u_ref)

    def clear(j, _):
        total[j] = jnp.zeros(total.shape[1:], F32)
        return 0

    lax.fori_loop(0, HALF_BLOCKS, clear, 0)

    def fetch(step, buffer):
        return copies((order_ref, window_ref, half_ref), packed_ref, v_ref, u_ref, sems, step, buffer)

    def work(step, buffer):
        found = []
        for pair in range(STEP_PAIRS):
            slots = [order_ref[step * STEP_SLOTS + 2 * pair + i] for i in range(2)]
            tiles = []
            for i, slot in enumerate(slots):
                at = 2 * pair + i
                window = window_ref[slot]
                mine = (column >= low_ref[slot]) & (column < high_ref[slot])
                residual = side_by_side([residual_ref[window], residual_ref[window + 1]])
                residual = jnp.where(mine, residual, 0.0)
                weights_v = side_by_side(v_ref[buffer, at]).astype(F32)
                weighted = jnp.concatenate([weights_v * residual[0:1], weights_v * residual[1:2]], axis=0).astype(BF16)
                tile = dot_nt(weighted, side_by_side(u_ref[buffer, at, half_ref[slot]]))
                real, imag = tile[:TILE], tile[TILE:]
                tiles.append(jnp.concatenate([real, imag], axis=1))
                tiles.append(jnp.concatenate([-imag, real], axis=1))
            found.append((slots, jnp.concatenate(tiles, axis=0).astype(BF16)))
        for pair, (slots, both) in enumerate(found):
            tables = jnp.concatenate([table_ref[row_ref[slot]] for slot in slots], axis=1)
            block = block_ref[step * STEP_PAIRS + pair]
            total[block] = total[block] + dot(tables, both)

    over_steps(steps_ref[0], fetch, work)

    rows_inverse(total, head_ref, twist_ref, tail_ref, out_ref, *lines)


def gradient_rows(scalars, table, residual, packed, rows):
    return pl.pallas_call(
        gradient_kernel,
        in_specs=[pl.BlockSpec(memory_space=pltpu.SMEM)] * 8 + [pl.BlockSpec(memory_space=pltpu.VMEM)] * 5 + [pl.BlockSpec(memory_space=pl.ANY)],
        out_specs=pl.BlockSpec(memory_space=pl.ANY),
        out_shape=jax.ShapeDtypeStruct((rows, SIDE), BF16),
        scratch_shapes=[pltpu.VMEM((HALF_BLOCKS, rows, 2 * RADIX), F32)] + slot_buffers() + [
            pltpu.SemaphoreType.DMA((BUFFERS, STEP_SLOTS, 2)),
            pltpu.VMEM((ROWS_STEP * ROW_PITCH, RADIX), F32),
            pltpu.VMEM((ROWS_STEP * ROW_PITCH, RADIX), F32),
            pltpu.VMEM((2, ROWS_STEP, SIDE), BF16),
            pltpu.SemaphoreType.DMA((2,)),
        ],
        compiler_params=pltpu.CompilerParams(vmem_limit_bytes=31 * MIB),
        cost_estimate=pl.CostEstimate(flops=scalars[0].shape[0] * RADIX ** 3 * 8, bytes_accessed=96 * MIB, transcendentals=0),
        name="gradient",
    )(*scalars, table, residual, *inverse_tables(), packed)


def column_tables(first_row, rows):
    y = first_row + jnp.arange(rows, dtype=jnp.int32)
    r = jnp.arange(TILE_ROWS, dtype=jnp.int32)
    a = jnp.arange(TILE, dtype=jnp.int32)
    coarse = (r[:, None] * y[None, :] % TILE_ROWS).astype(F32) * (2.0 * math.pi / TILE_ROWS)
    fine = (a[:, None] * y[None, :] % SIDE).astype(F32) * (2.0 * math.pi / SIDE)
    coarse_cos, coarse_sin = jnp.cos(coarse), jnp.sin(coarse)
    fine_cos, fine_sin = jnp.cos(fine) / RADIX, jnp.sin(fine) / RADIX
    with_cos = jnp.concatenate([fine_cos, fine_sin])
    with_sin = jnp.concatenate([fine_sin, -fine_cos])
    forward = coarse_cos[:, None, :] * with_cos[None] - coarse_sin[:, None, :] * with_sin[None]
    inverse = coarse_cos[:, :, None] * with_cos.T[None] - coarse_sin[:, :, None] * with_sin.T[None]
    return lax.optimization_barrier((forward.astype(BF16), inverse.astype(BF16)))


def firsts(counts):
    slot = jnp.arange(counts.shape[1], dtype=jnp.int32)
    ahead = slot[None, None, :] < slot[None, :, None]
    return jnp.sum(jnp.where(ahead, counts[:, None, :], 0), axis=2)


def spread(values, band_count):
    return lax.all_to_all(jnp.broadcast_to(values[None], (band_count,) + values.shape), "band", 0, 0, tiled=True)


def on_device(sky_image, tile_band, tile_place, counts, kernel, observed):
    band_count = lax.axis_size("band")
    rows = sky_image.shape[0]
    slots_here = tile_place.shape[0]
    slots_all = band_count * slots_here
    tiles_across = sky_image.shape[1] // 2 // band_count // TILE
    tiles_here = slots_here // 2

    tile_row = tile_place // tiles_across
    tile_col = tile_band[:, 0] * tiles_across + tile_place % tiles_across
    first = firsts(counts)[0]
    packed = lax.all_gather(pack(first, kernel, tiles_here), "band", tiled=True)
    seen = line_up(first, observed, tiles_here)

    every = spread(jnp.stack([tile_row, tile_col, counts[0]]), band_count)
    all_row, all_col = (every[:, i].reshape(slots_all) for i in range(2))
    all_block = all_col // 2
    all_first = firsts(every[:, 2])
    all_window = jnp.minimum(all_first // VIS_SLOT, tiles_here - 2)
    all_low = all_first - all_window * VIS_SLOT
    all_high = (all_low + every[:, 2]).reshape(slots_all)
    all_low = all_low.reshape(slots_all)
    all_window = (all_window + tiles_here * jnp.arange(band_count, dtype=jnp.int32)[:, None]).reshape(slots_all)

    spectrum = rows_forward(sky_image)
    forward_table, inverse_table = column_tables(lax.axis_index("band").astype(jnp.int32) * rows, rows)

    slot = jnp.arange(slots_all, dtype=jnp.int32)
    block = jnp.arange(HALF_BLOCKS, dtype=jnp.int32)
    in_block = jnp.sum((all_block[:, None] == block[None, :]).astype(jnp.int32), axis=0)
    pairs_of = (in_block + 1) // 2
    pairs_to = jnp.sum(jnp.where(block[None, :] <= block[:, None], pairs_of[None, :], 0), axis=1)
    rank = jnp.sum(((all_block[:, None] == all_block[None, :]) & (slot[None, :] < slot[:, None])).astype(jnp.int32), axis=1)
    first_pair = jnp.sum(jnp.where(block[None, :] < all_block[:, None], pairs_of[None, :], 0), axis=1)
    position = 2 * first_pair + rank
    positions_most = (slots_all + HALF_BLOCKS + TILES_SLOTS - 1) // TILES_SLOTS * TILES_SLOTS
    positions = jnp.arange(positions_most, dtype=jnp.int32)
    order = slots_all + jnp.sum(jnp.where(position[None, :] == positions[:, None], slot[None, :] - slots_all, 0), axis=1)
    pair_block = jnp.sum((pairs_to[None, :] <= positions[:positions_most // 2, None]).astype(jnp.int32), axis=1)
    pair_block = jnp.minimum(pair_block, HALF_BLOCKS - 1)
    steps = (pairs_to[-1:] + STEP_PAIRS - 1) // STEP_PAIRS

    def spare(values):
        return jnp.pad(values, (0, 8))

    scalars = (order, spare(all_window), spare(all_low), spare(all_high), spare(all_row), spare(all_col % 2), pair_block, steps)
    tiles = tile_parts(scalars, forward_table, spectrum)
    parts = model_parts(scalars, packed, tiles).reshape(band_count, slots_here, VIS_SLOT)
    model = jnp.sum(lax.all_to_all(parts.astype(BF16), "band", 0, 0, tiled=True).astype(F32), axis=0)
    residual = seen.reshape(slots_here, VIS_SLOT) - model
    residual = spread(residual.astype(BF16), band_count).astype(F32).reshape(band_count * tiles_here, 2, VIS_SLOT)
    return gradient_rows(scalars, inverse_table, residual, packed, rows)


def solution(mesh):
    return jax.shard_map(
        on_device,
        mesh=mesh,
        in_specs=(
            P(("parts", "band"), None),
            P(("parts", "band"), None),
            P(("parts", "band")),
            P(("parts", "band"), None),
            P(("parts", "band"), None, None),
            P(("parts", "band"), None, None),
        ),
        out_specs=P(("parts", "band"), None),
        check_vma=False,
    )
```
